256 devices in a mesh: dp: 8 (over x, y_lo), mp: 32 (over y_hi, z, core).
Axes of the slice: x: 4, y: 4 (y_hi: 2, y_lo: 2; y = y_hi * 2 + y_lo), z: 8, core: 2. Of those that a mesh axis runs over, the one named last changes fastest.
Arguments:
- block_in: bfloat16 [2048, 6144], P(('dp', 'mp')), may hold values from -6 to 6
- norm_gain: float32 [6144], replicated, may hold values from 0.5 to 1.5
- weight_in: bfloat16 [6144, 12288], P(None, 'mp'), may hold values from -0.078125 to 0.078125
- weight_out: bfloat16 [12288, 6144], P('mp'), may hold values from -0.0546875 to 0.0546875
- output_grad: bfloat16 [2048, 6144], P(('dp', 'mp')), may hold values from -24 to 24
Outputs:
- mixed: bfloat16 [2048, 6144], P(('dp', 'mp'))
- input_grad: bfloat16 [2048, 6144], P(('dp', 'mp'))
- grad_in: float32 [6144, 12288], P('dp', 'mp')
- grad_out: float32 [12288, 6144], P('mp', 'dp')
The draws below stay inside these ranges and needn't reach their ends.
All inputs are finite; a program needn't handle non-finite values.
Results may differ from the reference program's by a relative error of at most 0.02.
Values may be sent and summed in bfloat16 or wider, within the bound.
A program may use at most 128 MiB of HBM per device.

```python
import jax
import jax.numpy as jnp
from jax import lax

D = 6144
FF = 12288
TOK_GRP = 256
TOKENS = 2048
N_DP = 8
N_MP = 32


def with_spikes(array, own_key, source, target, parts, factor):
    def block_of(dim):
        return (jnp.arange(array.shape[dim]) // (array.shape[dim] // parts)).reshape((-1,) + (1,) * (array.ndim - 1 - dim))

    first = jax.random.permutation(own_key, parts)[block_of(target)]
    other_side = (block_of(target) + parts // 2) % parts
    return jnp.where((block_of(source) == first) | (block_of(source) == other_side), factor * array, array)


def steps_of(own_key, extent, pieces, least, top_value):
    loudness, own = 1.0, jax.random.fold_in(own_key, 6)
    for position, blocks in pieces:
        draws = jnp.exp(jax.random.uniform(jax.random.fold_in(own, position), (blocks,), jnp.float32, least / len(pieces), top_value / len(pieces)))
        loudness = loudness * jnp.repeat(draws, extent[position] // blocks).reshape([-1 if axis == position else 1 for axis in range(len(extent))])
    return loudness


def normal_values(stream_key, dims, scale, bound, cuts=(), dtype=jnp.bfloat16):
    array = scale * jax.random.normal(stream_key, dims, jnp.float32)
    if cuts:
        array = array * steps_of(stream_key, dims, cuts, -0.22, 0.18)
    return jnp.clip(array, -bound, bound).astype(dtype)


def gaussian_with(key, extent, scale, most, cuts, heavy, kind=jnp.bfloat16):
    entries = scale * jax.random.normal(key, extent, jnp.float32)
    if cuts:
        entries = entries * steps_of(key, extent, cuts, -0.22, 0.18)
    return jnp.clip(with_spikes(entries, jax.random.fold_in(key, 3), *heavy), -most, most).astype(kind)


def setup_inputs(seed: int = 0) -> dict:
    splits = jax.random.split(jax.random.key(seed), 6)
    block_in = normal_values(splits[0], (TOKENS, D), 1.0, 6.0, ((0, 256),))
    norm_gain = jnp.clip(jax.random.uniform(splits[1], (D,), jnp.float32, 0.5, 1.5), 0.5, 1.5)
    weight_in = normal_values(splits[2], (D, FF), D ** -0.5, 0.078125, ((1, 32),))
    weight_out = normal_values(splits[3], (FF, D), FF ** -0.5, 0.0546875, ((0, 32),))
    output_grad = gaussian_with(splits[4], (TOKENS, D), 1.0, 24.0, ((0, 256),), (0, 1, 256, 6.0))
    return dict(block_in=block_in, norm_gain=norm_gain, weight_in=weight_in, weight_out=weight_out, output_grad=output_grad)


def normal_cdf(value):
    return 0.5 * (1.0 + lax.erf(value * 0.7071067811865476))

def group_sum(left, right):
    left_groups = left.reshape(N_DP, TOK_GRP, left.shape[1])
    right_groups = right.reshape(N_DP, TOK_GRP, right.shape[1])

    def add_group(total, pair):
        term = lax.dot_general(pair[0], pair[1], (((0,), (0,)), ((), ())), preferred_element_type=jnp.float32)
        term = lax.optimization_barrier(term.astype(jnp.bfloat16))
        return (total + term.astype(jnp.float32), None)
    start = jnp.zeros((left.shape[1], right.shape[1]), jnp.float32)
    total, unused = lax.scan(add_group, start, (left_groups, right_groups))
    return total

def block_sum(left_blocks, right_blocks, rows, cols):

    def add_block(total, pair):
        term = jnp.dot(pair[0], pair[1], preferred_element_type=jnp.float32)
        term = lax.optimization_barrier(term.astype(jnp.bfloat16))
        return (total + term.astype(jnp.float32), None)
    start = jnp.zeros((rows, cols), jnp.float32)
    total, unused = lax.scan(add_block, start, (left_blocks, right_blocks))
    return total

def reference(block_in, norm_gain, weight_in, weight_out, output_grad):
    width_block = FF // N_MP
    values = block_in.astype(jnp.float32)
    average = lax.optimization_barrier(jnp.mean(values, axis=1, keepdims=True))
    centred = values - average
    inv_scale = lax.rsqrt(lax.optimization_barrier(jnp.mean(centred * centred, axis=1, keepdims=True)) + 1e-06)
    standard = centred * inv_scale
    normed = (standard * norm_gain).astype(jnp.bfloat16)
    preact = jnp.dot(normed, weight_in, preferred_element_type=jnp.float32)
    hidden = (preact * normal_cdf(preact)).astype(jnp.bfloat16)
    hidden_blocks = jnp.moveaxis(hidden.reshape(TOKENS, N_MP, width_block), 1, 0)
    out_blocks = weight_out.reshape(N_MP, width_block, D)
    branch = block_sum(hidden_blocks, out_blocks, TOKENS, D)
    mixed = (values + branch).astype(jnp.bfloat16)
    hidden_grad = jnp.dot(output_grad, weight_out.T, preferred_element_type=jnp.float32)
    slope = normal_cdf(preact) + preact * jnp.exp(-0.5 * preact * preact) * 0.3989422804014327
    preact_grad = (hidden_grad * slope).astype(jnp.bfloat16)
    grad_blocks = jnp.moveaxis(preact_grad.reshape(TOKENS, N_MP, width_block), 1, 0)
    in_blocks = jnp.moveaxis(weight_in.T.reshape(N_MP, width_block, D), 0, 0)
    normed_grad = block_sum(grad_blocks, in_blocks, TOKENS, D)
    scaled = normed_grad * norm_gain
    input_grad = output_grad.astype(jnp.float32) + inv_scale * (scaled - lax.optimization_barrier(jnp.mean(scaled, axis=1, keepdims=True)) - standard * lax.optimization_barrier(jnp.mean(scaled * standard, axis=1, keepdims=True)))
    input_grad = input_grad.astype(jnp.bfloat16)
    grad_in = group_sum(normed, preact_grad)
    grad_out = group_sum(hidden, output_grad)
    return (mixed, input_grad, grad_in, grad_out)
```

```python
import jax
import jax.numpy as jnp
from jax import lax
from jax.experimental import pallas as pl
from jax.experimental.pallas import tpu as pltpu
from jax.sharding import PartitionSpec as P

MESH = pl.DeviceIdType.MESH
F32, BF16 = jnp.float32, jnp.bfloat16

NX, NZ = 4, 8
ROWS = 8
CHUNK = NX * ROWS
WIDE = 1536
UNITS = 384
BLOCK = 256
SEMS = 192


def place():
    dp, mp = lax.axis_index("dp"), lax.axis_index("mp")
    return (
        lax.div(dp, 2),
        lax.rem(dp, 2),
        lax.div(mp, 16),
        lax.rem(lax.div(mp, 2), NZ),
        lax.rem(mp, 2),
    )


def device(x, yl, yh, z, c):
    return (x * 2 + yl, (yh * NZ + z) * 2 + c)


def slot(way, dist):
    if dist == 0:
        return 0
    if dist == 4:
        return 7
    return 2 * dist - 1 + way


def on_ring(way, dist, h):
    return dist < 4 or way == h


def dot(left, right, dims=((1,), (0,))):
    return lax.dot_general(left, right, (dims, ((), ())), preferred_element_type=F32)


def kernel(
    x_ref, gain_ref, wi_any, wo_any, g_ref,
    mixed_ref, igrad_ref, gin_any, gout_any,
    wi, wo, std, msg, got, acts, cots,
    part, part_in, slope, hid, dpre, hid_t, dpre_t,
    prod, prod_sib, ring_in, ring_out, y_out, y_in, rows_out, rows_in,
    gsum, gsend, gin_got, gres, gturn,
    ssem, rsem, lsem,
):
    x, yl, yh, z, c = place()
    xs = [lax.rem(x + k, NX) for k in range(NX)]
    zp, zm = lax.rem(z + 1, NZ), lax.rem(z + NZ - 1, NZ)
    to_z = (device(x, yl, yh, zp, c), device(x, yl, yh, zm, c))
    to_sib = device(x, yl, yh, z, 1 - c)
    to_yh = device(x, yl, 1 - yh, z, c)
    to_yl = device(x, 1 - yl, yh, z, c)
    to_x = [device(xs[k], yl, yh, z, c) for k in range(NX)]

    barrier = pltpu.get_barrier_semaphore()
    for other in (*to_z, to_sib, to_yh, to_yl, *to_x[1:]):
        pl.semaphore_signal(barrier, inc=1, device_id=other, device_id_type=MESH)

    load_wi = pltpu.make_async_copy(
        wi_any.at[pl.ds(pl.multiple_of(x * WIDE, WIDE), WIDE)], wi, lsem.at[0])
    load_wo = pltpu.make_async_copy(
        wo_any.at[:, pl.ds(pl.multiple_of(x * WIDE, WIDE), WIDE)], wo, lsem.at[1])
    load_wi.start()
    load_wo.start()

    values = x_ref[...].astype(F32)
    average = jnp.mean(values, axis=1, keepdims=True)
    centred = values - average
    inv_scale = lax.rsqrt(jnp.mean(centred * centred, axis=1, keepdims=True) + 1e-06)
    standard = centred * inv_scale
    std[...] = standard
    normed = standard * gain_ref[...]
    grad = g_ref[...].astype(F32)
    for q in range(NX):
        cols = slice(q * WIDE, (q + 1) * WIDE)
        msg[q] = jnp.concatenate([normed[:, cols], grad[:, cols]], axis=0).astype(BF16)

    pl.semaphore_wait(barrier, 8)

    pending = []

    def send(src, dst, to):
        k = len(pending)
        copy = pltpu.make_async_remote_copy(
            src_ref=src, dst_ref=dst, send_sem=ssem.at[k], recv_sem=rsem.at[k],
            device_id=to, device_id_type=MESH)
        copy.start()
        pending.append(copy)
        return copy

    first = [send(msg.at[xs[k]], got.at[x], to_x[k]) for k in range(1, NX)]
    got[x] = msg[x]
    for copy in first:
        copy.wait_recv()
    pieces = [got[a].astype(F32) for a in range(NX)]
    acts[0] = jnp.concatenate([p[:ROWS] for p in pieces], axis=0).astype(BF16)
    cots[0] = jnp.concatenate([p[ROWS:] for p in pieces], axis=0).astype(BF16)

    class Gather:
        def __init__(self, buf):
            self.buf, self.ring, self.sib = buf, {}, {}

        def spread(self, way, dist, h):
            s = slot(way, dist)
            k = 4 * s + 2 * h
            for w in (0, 1) if dist == 0 else (way,):
                if dist < 4 and on_ring(w, dist + 1, h):
                    t = 4 * slot(w, dist + 1) + 2 * h
                    self.ring[w, dist + 1, h] = send(self.buf.at[k], self.buf.at[t], to_z[w])
            self.sib[s, h] = send(self.buf.at[k], self.buf.at[k + 1], to_sib)

        def start(self):
            self.y = send(self.buf.at[0], self.buf.at[2], to_yh)
            self.spread(0, 0, 0)

        def other(self):
            self.y.wait_recv()
            self.spread(0, 0, 1)

        def step(self, dist):
            for h in (0, 1):
                for way in (0, 1):
                    if on_ring(way, dist, h):
                        self.ring[way, dist, h].wait_recv()
                        self.spread(way, dist, h)

        def block(self, b):
            for s in (2 * b, 2 * b + 1):
                for h in (0, 1):
                    self.sib[s, h].wait_recv()
            return self.buf[8 * b:8 * b + 8].reshape(BLOCK, WIDE)

    class Across:
        def __init__(self, i, result):
            self.part, self.came, self.result = part.at[i], part_in.at[i], result
            self.out, self.back = {}, {}

        def give(self, b, term):
            self.part[b] = term.astype(BF16).reshape(NX, BLOCK // NX, UNITS)
            self.out[b] = [
                send(self.part.at[b, xs[k]], self.came.at[b, k - 1], to_x[k]) for k in range(1, NX)]

        def total(self, b):
            for copy in self.out[b]:
                copy.wait_recv()
            total = self.part[b, x].astype(F32)
            for k in range(NX - 1):
                total = total + self.came[b, k].astype(F32)
            return total

        def share(self, b, value):
            self.result[b, x] = value.astype(BF16)
            self.back[b] = [
                send(self.result.at[b, x], self.result.at[b, x], to_x[k]) for k in range(1, NX)]

        def whole(self, b):
            for copy in self.back[b]:
                copy.wait_recv()
            return self.result[b].reshape(BLOCK, UNITS)

    class Scatter:
        def __init__(self, i):
            self.prod, self.sib = prod.at[i], prod_sib.at[i]
            self.rin, self.rout = ring_in.at[i], ring_out.at[i]
            self.yout, self.yin = y_out.at[i], y_in.at[i]
            self.xout, self.xin = rows_out.at[i], rows_in.at[i]
            self.sibs, self.ring, self.seen = {}, {}, set()

        def give(self, b, left, right, dims):
            for n in range(0, WIDE, 512):
                if dims == 1:
                    term = dot(left, right[n:n + 512, :], ((1,), (1,)))
                else:
                    term = dot(left, right[:, n:n + 512])
                term = term.astype(BF16).reshape(4, 2, CHUNK, 512)
                for core in (0, 1):
                    self.prod[core, 4 * b:4 * b + 4, :, n:n + 512] = term[:, core]
            rows = pl.ds(4 * b, 4)
            self.sibs[b] = send(self.prod.at[1, rows], self.sib.at[rows], to_sib)

        def term(self, s, h):
            if s // 2 not in self.seen:
                self.seen.add(s // 2)
                self.sibs[s // 2].wait_recv()
            q = 2 * s + h
            return self.prod[0, q].astype(F32) + self.sib[q].astype(F32)

        def hop(self, way, dist, h):
            value = self.term(slot(way, dist), h)
            if (way, dist, h) in self.ring:
                self.ring[way, dist, h].wait_recv()
                value = value + self.rin[way, dist, h].astype(F32)
            self.rout[way, dist - 1, h] = value.astype(BF16)
            self.ring[way, dist - 1, h] = send(
                self.rout.at[way, dist - 1, h], self.rin.at[way, dist - 1, h], to_z[1 - way])

        def near(self, h):
            value = self.term(0, h)
            for way in (0, 1):
                self.ring[way, 0, h].wait_recv()
                value = value + self.rin[way, 0, h].astype(F32)
            return value

        def cross(self):
            self.yout[...] = self.near(1).astype(BF16)
            self.y = send(self.yout, self.yin, to_yh)

        def rows(self):
            value = self.near(0)
            self.y.wait_recv()
            value = value + self.yin[...].astype(F32)
            self.xout[...] = value.reshape(NX, ROWS, WIDE)
            self.x = [send(self.xout.at[xs[k]], self.xin.at[x], to_x[k]) for k in range(1, NX)]
            self.xin[x] = self.xout[x]

        def done(self):
            for copy in self.x:
                copy.wait_recv()
            return [self.xin[a] for a in range(NX)]

    class Weights:
        def __init__(self, i):
            self.sum, self.out, self.came = gsum.at[i], gsend.at[i], gin_got.at[i]

        def give(self, left_t, right):
            left = left_t[...]
            for n in range(4):
                cols = slice(n * UNITS, (n + 1) * UNITS)
                term = dot(left, right[:, :, cols].reshape(4 * BLOCK, UNITS))
                self.sum[n // 2, :, (n % 2) * UNITS:(n % 2 + 1) * UNITS] = term
            self.out[...] = self.sum[1 - yl].astype(BF16)
            self.copy = send(self.out, self.came, to_yl)

        def total(self):
            self.copy.wait_recv()
            return self.sum[yl] + self.came[...].astype(F32)

    ga, gg = Gather(acts), Gather(cots)
    fwd, bwd = Across(0, hid), Across(1, dpre)
    out, back = Scatter(0), Scatter(1)
    w_out, w_in = Weights(0), Weights(1)

    def pre(b):
        fwd.give(b, dot(ga.block(b), wi[...]))

    def act(b):
        value = fwd.total(b)
        cdf = 0.5 * (1.0 + lax.erf(value * 0.7071067811865476))
        slope[b] = cdf + value * jnp.exp(-0.5 * value * value) * 0.3989422804014327
        fwd.share(b, value * cdf)

    def cot(b):
        bwd.give(b, dot(gg.block(b), wo[...], ((1,), (1,))))

    def act_back(b):
        bwd.share(b, bwd.total(b) * slope[b])

    def branch(b):
        value = fwd.whole(b)
        hid_t[:, b * BLOCK:(b + 1) * BLOCK] = value.T
        out.give(b, value, wo, 0)

    def back_prod(b):
        value = bwd.whole(b)
        dpre_t[:, b * BLOCK:(b + 1) * BLOCK] = value.T
        back.give(b, value, wi, 1)

    ga.start()
    ga.other()
    ga.step(1)
    load_wi.wait()
    load_wo.wait()
    pre(0)
    ga.step(2)
    pre(1)
    act(0)
    ga.step(3)
    gg.start()
    pre(2)
    act(1)
    ga.step(4)
    gg.other()
    pre(3)
    act(2)
    gg.step(1)
    act(3)
    cot(0)
    branch(0)
    gg.step(2)
    cot(1)
    act_back(0)
    branch(1)
    branch(2)
    gg.step(3)
    branch(3)
    out.hop(0, 4, 0)
    out.hop(1, 4, 1)
    out.hop(0, 3, 1)
    out.hop(1, 3, 0)
    cot(2)
    act_back(1)
    gg.step(4)
    cot(3)
    act_back(2)
    out.hop(0, 3, 0)
    out.hop(1, 3, 1)
    back_prod(0)
    out.hop(0, 2, 1)
    out.hop(1, 2, 0)
    act_back(3)
    back_prod(1)
    out.hop(0, 2, 0)
    out.hop(1, 2, 1)
    back_prod(2)
    out.hop(0, 1, 1)
    out.hop(1, 1, 0)
    back_prod(3)
    out.hop(0, 1, 0)
    out.hop(1, 1, 1)
    back.hop(0, 4, 0)
    back.hop(1, 4, 1)
    back.hop(0, 3, 1)
    back.hop(1, 3, 0)
    out.cross()
    w_out.give(hid_t, cots)
    back.hop(0, 3, 0)
    back.hop(1, 3, 1)
    out.rows()
    back.hop(0, 2, 1)
    back.hop(1, 2, 0)
    w_in.give(dpre_t, acts)
    back.hop(0, 2, 0)
    back.hop(1, 2, 1)
    gres[...] = w_out.total()
    store_out = pltpu.make_async_copy(gres, gout_any, lsem.at[2])
    store_out.start()
    back.hop(0, 1, 1)
    back.hop(1, 1, 0)
    for a, piece in enumerate(out.done()):
        cols = slice(a * WIDE, (a + 1) * WIDE)
        mixed_ref[:, cols] = (x_ref[:, cols].astype(F32) + piece).astype(BF16)
    back.hop(0, 1, 0)
    back.hop(1, 1, 1)
    back.cross()
    grad_in_t = w_in.total()
    back.rows()
    gturn[...] = grad_in_t.T
    store_in = pltpu.make_async_copy(gturn, gin_any, lsem.at[3])
    store_in.start()

    scaled = [p * gain_ref[:, a * WIDE:(a + 1) * WIDE] for a, p in enumerate(back.done())]
    standards = [std[:, a * WIDE:(a + 1) * WIDE] for a in range(NX)]
    mean_scaled = sum(jnp.sum(s, axis=1, keepdims=True) for s in scaled) / x_ref.shape[1]
    mean_both = sum(
        jnp.sum(s * t, axis=1, keepdims=True) for s, t in zip(scaled, standards)) / x_ref.shape[1]
    for a in range(NX):
        cols = slice(a * WIDE, (a + 1) * WIDE)
        change = inv_scale * (scaled[a] - mean_scaled - standards[a] * mean_both)
        igrad_ref[:, cols] = (g_ref[:, cols].astype(F32) + change).astype(BF16)

    for copy in pending:
        copy.wait_send()
    store_out.wait()
    store_in.wait()


def local(block_in, norm_gain, weight_in, weight_out, output_grad):
    vmem, hbm = pl.BlockSpec(memory_space=pltpu.VMEM), pl.BlockSpec(memory_space=pl.ANY)
    rows, width = block_in.shape
    half = 2 * UNITS

    def buf(*shape, dtype=BF16):
        return pltpu.VMEM(shape, dtype)

    quarter = BLOCK // NX
    scratch = dict(
        wi=buf(WIDE, UNITS), wo=buf(UNITS, WIDE), std=buf(rows, width, dtype=F32),
        msg=buf(NX, 2 * ROWS, WIDE), got=buf(NX, 2 * ROWS, WIDE),
        acts=buf(32, CHUNK, WIDE), cots=buf(32, CHUNK, WIDE),
        part=buf(2, 4, NX, quarter, UNITS), part_in=buf(2, 4, NX - 1, quarter, UNITS),
        slope=buf(4, quarter, UNITS, dtype=F32),
        hid=buf(4, NX, quarter, UNITS), dpre=buf(4, NX, quarter, UNITS),
        hid_t=buf(UNITS, 4 * BLOCK), dpre_t=buf(UNITS, 4 * BLOCK),
        prod=buf(2, 2, 16, CHUNK, WIDE), prod_sib=buf(2, 16, CHUNK, WIDE),
        ring_in=buf(2, 2, 4, 2, CHUNK, WIDE), ring_out=buf(2, 2, 4, 2, CHUNK, WIDE),
        y_out=buf(2, CHUNK, WIDE), y_in=buf(2, CHUNK, WIDE),
        rows_out=buf(2, NX, ROWS, WIDE, dtype=F32), rows_in=buf(2, NX, ROWS, WIDE, dtype=F32),
        gsum=buf(2, 2, UNITS, half, dtype=F32), gsend=buf(2, UNITS, half),
        gin_got=buf(2, UNITS, half), gres=buf(UNITS, half, dtype=F32),
        gturn=buf(half, UNITS, dtype=F32),
        ssem=pltpu.SemaphoreType.DMA((SEMS,)), rsem=pltpu.SemaphoreType.DMA((SEMS,)),
        lsem=pltpu.SemaphoreType.DMA((4,)),
    )
    return pl.pallas_call(
        kernel,
        name="block",
        out_shape=(
            jax.ShapeDtypeStruct((rows, width), BF16),
            jax.ShapeDtypeStruct((rows, width), BF16),
            jax.ShapeDtypeStruct((half, UNITS), F32),
            jax.ShapeDtypeStruct((UNITS, half), F32),
        ),
        in_specs=[vmem, vmem, hbm, hbm, vmem],
        out_specs=(vmem, vmem, hbm, hbm),
        scratch_shapes=list(scratch.values()),
        compiler_params=pltpu.CompilerParams(
            collective_id=0, has_side_effects=True, vmem_limit_bytes=58 * 2**20
        ),
    )(block_in, norm_gain.reshape(1, width), weight_in, weight_out, output_grad)


def solution(mesh):
    in_specs = (P(("dp", "mp"), None), P(), P(None, "mp"), P("mp", None), P(("dp", "mp"), None))
    out_specs = (P(("dp", "mp"), None), P(("dp", "mp"), None), P("dp", "mp"), P("mp", "dp"))
    return jax.shard_map(local, mesh=mesh, in_specs=in_specs, out_specs=out_specs, check_vma=False)
```

```python
import jax
import jax.numpy as jnp
from jax import lax
from jax.experimental import pallas as pl
from jax.experimental.pallas import tpu as pltpu
from jax.sharding import PartitionSpec as P

MESH = pl.DeviceIdType.MESH
F32, BF16 = jnp.float32, jnp.bfloat16

NX, NZ = 4, 8
ROWS = 8
CHUNK = NX * ROWS
WIDE = 1536
UNITS = 384
BLOCK = 256
HALF = CHUNK // 2
PER = BLOCK // (4 * HALF)
FAR = 3
SEMS = 320


def place():
    dp, mp = lax.axis_index("dp"), lax.axis_index("mp")
    return (
        lax.div(dp, 2),
        lax.rem(dp, 2),
        lax.div(mp, 16),
        lax.rem(lax.div(mp, 2), NZ),
        lax.rem(mp, 2),
    )


def device(x, yl, yh, z, c):
    return (x * 2 + yl, (yh * NZ + z) * 2 + c)


def slot(way, dist):
    if dist == 0:
        return 0
    if dist == 4:
        return 7
    return 2 * dist - 1 + way


def dot(left, right, dims=((1,), (0,))):
    return lax.dot_general(left, right, (dims, ((), ())), preferred_element_type=F32)


def kernel(
    x_ref, gain_ref, wi_any, wo_any, g_ref,
    mixed_ref, igrad_ref, gin_any, gout_any,
    wi, wo, std, msg, got, acts, cots,
    terms, terms_in, slope, hid, dpre, hid_t, dpre_t,
    prod, prod_sib, ring_in, ring_out, y_out, y_in, rows_out, rows_in,
    gsum, gsend, gin_got, gres, gturn,
    ssem, rsem, lsem,
):
    x, yl, yh, z, c = place()
    xs = [lax.rem(x + k, NX) for k in range(NX)]
    zp, zm = lax.rem(z + 1, NZ), lax.rem(z + NZ - 1, NZ)
    to_z = (device(x, yl, yh, zp, c), device(x, yl, yh, zm, c))
    to_sib = device(x, yl, yh, z, 1 - c)
    to_yh = device(x, yl, 1 - yh, z, c)
    to_yl = device(x, 1 - yl, yh, z, c)
    to_x = [device(xs[k], yl, yh, z, c) for k in range(NX)]

    barrier = pltpu.get_barrier_semaphore()
    for other in (*to_z, to_sib, to_yh, to_yl, *to_x[1:]):
        pl.semaphore_signal(barrier, inc=1, device_id=other, device_id_type=MESH)

    load_wi = pltpu.make_async_copy(
        wi_any.at[pl.ds(pl.multiple_of(x * WIDE, WIDE), WIDE)], wi, lsem.at[0])
    load_wo = pltpu.make_async_copy(
        wo_any.at[:, pl.ds(pl.multiple_of(x * WIDE, WIDE), WIDE)], wo, lsem.at[1])
    load_wi.start()
    load_wo.start()

    values = x_ref[...].astype(F32)
    average = jnp.mean(values, axis=1, keepdims=True)
    centred = values - average
    inv_scale = lax.rsqrt(jnp.mean(centred * centred, axis=1, keepdims=True) + 1e-06)
    standard = centred * inv_scale
    std[...] = standard
    normed = standard * gain_ref[...]
    grad = g_ref[...].astype(F32)
    for q in range(NX):
        cols = slice(q * WIDE, (q + 1) * WIDE)
        msg[q] = jnp.concatenate([normed[:, cols], grad[:, cols]], axis=0).astype(BF16)

    pl.semaphore_wait(barrier, 8)

    pending = []

    def send(src, dst, to):
        k = len(pending)
        copy = pltpu.make_async_remote_copy(
            src_ref=src, dst_ref=dst, send_sem=ssem.at[k], recv_sem=rsem.at[k],
            device_id=to, device_id_type=MESH)
        copy.start()
        pending.append(copy)
        return copy

    first = [send(msg.at[xs[k]], got.at[x], to_x[k]) for k in range(1, NX)]
    got[x] = msg[x]
    for copy in first:
        copy.wait_recv()
    pieces = [got[a].astype(F32) for a in range(NX)]
    for part in (0, 1):
        pair = pieces[2 * part:2 * part + 2]
        acts[part, 0] = jnp.concatenate([p[:ROWS] for p in pair], axis=0).astype(BF16)
        cots[part, 0] = jnp.concatenate([p[ROWS:] for p in pair], axis=0).astype(BF16)

    def ways(dist, part, turn):
        return (0, 1) if dist < 4 else (part ^ turn,)

    class Gather:
        def __init__(self, buf, turn):
            self.buf, self.turn = buf, turn
            self.near, self.ring, self.y, self.sib = {}, {}, {}, {}

        def at(self, part, s, h):
            return self.buf.at[part, 4 * s + h]

        def pass_on(self, part, way, dist, h):
            here = self.at(part, slot(way, dist), h)
            if dist < (FAR - 1 if h else 4) and way in ways(dist + 1, part, self.turn):
                there = self.at(part, slot(way, dist + 1), h)
                self.ring[part, way, dist + 1, h] = send(here, there, to_z[way])
            if dist >= FAR and h == 0:
                there = self.at(part, slot(way, dist), 1)
                self.y[part, way, dist] = send(here, there, to_yh)

        def to_core(self, part, s):
            self.sib[part, s] = send(
                self.buf.at[part, pl.ds(4 * s, 2)], self.buf.at[part, pl.ds(4 * s + 2, 2)], to_sib)

        def start(self, part):
            self.near[part] = send(self.at(part, 0, 0), self.at(part, 0, 1), to_yh)
            for way in (0, 1):
                self.pass_on(part, way, 0, 0)

        def other(self, part):
            self.near[part].wait_recv()
            for way in (0, 1):
                self.pass_on(part, way, 0, 1)
            self.to_core(part, 0)

        def own(self, part, dist):
            for way in ways(dist, part, self.turn):
                self.ring[part, way, dist, 0].wait_recv()
                self.pass_on(part, way, dist, 0)

        def oth(self, part, dist):
            for way in (0, 1):
                self.ring[part, way, dist, 1].wait_recv()
                self.pass_on(part, way, dist, 1)
                self.to_core(part, slot(way, dist))

        def far(self, part, dist):
            for way in ways(dist, part, self.turn):
                self.y[part, way, dist].wait_recv()
                self.to_core(part, slot(way, dist))

        def block(self, part, b):
            for s in range(PER * b, PER * b + PER):
                self.sib[part, s].wait_recv()
            return self.buf[part, 4 * PER * b:4 * PER * (b + 1)].reshape(BLOCK, WIDE)

    class Across:
        def __init__(self, i, result):
            self.term, self.came, self.result = terms.at[i], terms_in.at[i], result
            self.out, self.back = {}, {}

        def give(self, b, term):
            self.term[b] = term.astype(BF16).reshape(NX, BLOCK // NX, UNITS)
            self.out[b] = [
                send(self.term.at[b, xs[k]], self.came.at[b, k - 1], to_x[k]) for k in range(1, NX)]

        def total(self, b):
            for copy in self.out[b]:
                copy.wait_recv()
            total = self.term[b, x].astype(F32)
            for k in range(NX - 1):
                total = total + self.came[b, k].astype(F32)
            return total

        def share(self, b, value):
            self.result[b, x] = value.astype(BF16)
            self.back[b] = [
                send(self.result.at[b, x], self.result.at[b, x], to_x[k]) for k in range(1, NX)]

        def whole(self, b):
            for copy in self.back[b]:
                copy.wait_recv()
            return self.result[b].reshape(BLOCK, UNITS)

    class Scatter:
        def __init__(self, i, turn):
            self.turn = turn
            self.prod, self.sib = prod.at[i], prod_sib.at[i]
            self.rin, self.rout = ring_in.at[i], ring_out.at[i]
            self.yout, self.yin = y_out.at[i], y_in.at[i]
            self.xout, self.xin = rows_out.at[i], rows_in.at[i]
            self.sibs, self.ring, self.y, self.seen = {}, {}, {}, set()

        def give(self, k, left, right, dims):
            for n in range(0, WIDE, 512):
                if dims == 1:
                    term = dot(left, right[n:n + 512, :], ((1,), (1,)))
                else:
                    term = dot(left, right[:, n:n + 512])
                term = term.astype(BF16).reshape(PER, 2, 2, HALF, 512)
                for core in (0, 1):
                    self.prod[core, k, :, :, n:n + 512] = term[:, core].reshape(2 * PER, HALF, 512)
            self.sibs[k] = send(self.prod.at[1, k], self.sib.at[k], to_sib)

        def term(self, part, s, h):
            k, q = 2 * part + s // PER, 2 * (s % PER) + h
            if k not in self.seen:
                self.seen.add(k)
                self.sibs[k].wait_recv()
            return self.prod[0, k, q].astype(F32) + self.sib[k, q].astype(F32)

        def hop(self, part, way, dist, h):
            value = self.term(part, slot(way, dist), h)
            if (part, way, dist, h) in self.ring:
                self.ring[part, way, dist, h].wait_recv()
                value = value + self.rin[part, way, dist, h].astype(F32)
            self.rout[part, way, dist - 1, h] = value.astype(BF16)
            self.ring[part, way, dist - 1, h] = send(
                self.rout.at[part, way, dist - 1, h], self.rin.at[part, way, dist - 1, h],
                to_z[1 - way])

        def hops(self, part, dist, h):
            for way in ways(dist, part, self.turn):
                self.hop(part, way, dist, h)

        def near(self, part, h):
            value = self.term(part, 0, h)
            for way in (0, 1):
                self.ring[part, way, 0, h].wait_recv()
                value = value + self.rin[part, way, 0, h].astype(F32)
            return value

        def cross(self, part):
            self.yout[part] = self.near(part, 1).astype(BF16)
            self.y[part] = send(self.yout.at[part], self.yin.at[part], to_yh)

        def rows(self, part):
            value = self.near(part, 0)
            self.y[part].wait_recv()
            value = value + self.yin[part].astype(F32)
            self.xout[2 * part:2 * part + 2] = value.reshape(2, ROWS, WIDE)

        def across(self):
            self.x = [send(self.xout.at[xs[k]], self.xin.at[x], to_x[k]) for k in range(1, NX)]
            self.xin[x] = self.xout[x]

        def done(self):
            for copy in self.x:
                copy.wait_recv()
            return [self.xin[a] for a in range(NX)]

    class Weights:
        def __init__(self, i):
            self.sum, self.out, self.came = gsum.at[i], gsend.at[i], gin_got.at[i]

        def give(self, left_t, right):
            left = left_t[...]
            for n in range(4):
                cols = slice(n * UNITS, (n + 1) * UNITS)
                term = dot(left, right[:, :, :, cols].reshape(4 * BLOCK, UNITS))
                self.sum[n // 2, :, (n % 2) * UNITS:(n % 2 + 1) * UNITS] = term
            self.out[...] = self.sum[1 - yl].astype(BF16)
            self.copy = send(self.out, self.came, to_yl)

        def total(self):
            self.copy.wait_recv()
            return self.sum[yl] + self.came[...].astype(F32)

    ga, gg = Gather(acts, 0), Gather(cots, 1)
    fwd, bwd = Across(0, hid), Across(1, dpre)
    out, back = Scatter(0, 0), Scatter(1, 1)
    w_out, w_in = Weights(0), Weights(1)

    def pre(part, b):
        fwd.give(2 * part + b, dot(ga.block(part, b), wi[...]))

    def act(part, b):
        k = 2 * part + b
        value = fwd.total(k)
        cdf = 0.5 * (1.0 + lax.erf(value * 0.7071067811865476))
        slope[k] = cdf + value * jnp.exp(-0.5 * value * value) * 0.3989422804014327
        fwd.share(k, value * cdf)

    def cot(part, b):
        bwd.give(2 * part + b, dot(gg.block(part, b), wo[...], ((1,), (1,))))

    def act_back(part, b):
        k = 2 * part + b
        bwd.share(k, bwd.total(k) * slope[k])

    def branch(part, b):
        k = 2 * part + b
        value = fwd.whole(k)
        hid_t[:, k * BLOCK:(k + 1) * BLOCK] = value.T
        out.give(k, value, wo, 0)

    def back_prod(part, b):
        k = 2 * part + b
        value = bwd.whole(k)
        dpre_t[:, k * BLOCK:(k + 1) * BLOCK] = value.T
        back.give(k, value, wi, 1)

    def mixed():
        for a, piece in enumerate(out.done()):
            cols = slice(a * WIDE, (a + 1) * WIDE)
            mixed_ref[:, cols] = (x_ref[:, cols].astype(F32) + piece).astype(BF16)

    def store_out_grad():
        gres[...] = w_out.total()
        store_out.start()

    def store_in_grad():
        gturn[...] = w_in.total().T
        store_in.start()

    def finish():
        scaled = [p * gain_ref[:, a * WIDE:(a + 1) * WIDE] for a, p in enumerate(back.done())]
        standards = [std[:, a * WIDE:(a + 1) * WIDE] for a in range(NX)]
        mean_scaled = sum(jnp.sum(s, axis=1, keepdims=True) for s in scaled) / x_ref.shape[1]
        mean_both = sum(
            jnp.sum(s * t, axis=1, keepdims=True)
            for s, t in zip(scaled, standards)) / x_ref.shape[1]
        for a in range(NX):
            cols = slice(a * WIDE, (a + 1) * WIDE)
            change = inv_scale * (scaled[a] - mean_scaled - standards[a] * mean_both)
            igrad_ref[:, cols] = (g_ref[:, cols].astype(F32) + change).astype(BF16)

    store_out = pltpu.make_async_copy(gres, gout_any, lsem.at[2])
    store_in = pltpu.make_async_copy(gturn, gin_any, lsem.at[3])

    ga.start(0)
    ga.start(1)
    ga.own(0, 1)
    ga.other(0)
    ga.own(1, 1)
    ga.other(1)
    ga.own(0, 2)
    ga.oth(0, 1)
    gg.start(0)
    ga.own(1, 2)
    gg.start(1)
    ga.oth(1, 1)
    ga.own(0, 3)
    ga.oth(0, 2)
    load_wi.wait()
    load_wo.wait()
    pre(0, 0)
    gg.other(0)
    gg.own(0, 1)
    ga.own(1, 3)
    gg.other(1)
    gg.own(1, 1)
    ga.far(0, 3)
    ga.oth(1, 2)
    ga.own(0, 4)
    gg.oth(0, 1)
    act(0, 0)
    ga.far(1, 3)
    gg.own(0, 2)
    pre(1, 0)
    ga.own(1, 4)
    gg.oth(1, 1)
    ga.far(0, 4)
    gg.own(1, 2)
    pre(0, 1)
    branch(0, 0)
    ga.far(1, 4)
    act(1, 0)
    gg.own(0, 3)
    gg.oth(1, 2)
    gg.own(1, 3)
    pre(1, 1)
    cot(1, 0)
    gg.own(0, 4)
    gg.own(1, 4)
    branch(1, 0)
    gg.far(0, 3)
    act(0, 1)
    gg.oth(0, 2)
    act(1, 1)
    gg.far(1, 3)
    cot(0, 0)
    act_back(1, 0)
    gg.far(1, 4)
    gg.far(0, 4)
    branch(0, 1)
    cot(0, 1)
    cot(1, 1)
    branch(1, 1)
    w_out.give(hid_t, cots)
    out.hops(1, 4, 1)
    out.hops(1, 4, 0)
    out.hops(0, 4, 0)
    out.hops(0, 4, 1)
    act_back(0, 0)
    back_prod(1, 0)
    act_back(0, 1)
    out.hops(0, 3, 0)
    act_back(1, 1)
    out.hops(0, 3, 1)
    out.hops(1, 3, 1)
    out.hops(1, 3, 0)
    back_prod(0, 0)
    out.hops(0, 2, 0)
    back_prod(0, 1)
    out.hops(0, 2, 1)
    out.hops(1, 2, 1)
    back_prod(1, 1)
    back.hops(0, 4, 1)
    back.hops(0, 4, 0)
    out.hops(0, 1, 0)
    out.hops(0, 1, 1)
    back.hops(1, 4, 1)
    out.hops(1, 2, 0)
    out.hops(1, 1, 1)
    back.hops(1, 4, 0)
    w_in.give(dpre_t, acts)
    back.hops(0, 3, 0)
    back.hops(0, 3, 1)
    store_out_grad()
    back.hops(1, 3, 1)
    back.hops(1, 3, 0)
    out.hops(1, 1, 0)
    back.hops(0, 2, 1)
    back.hops(1, 2, 1)
    back.hops(1, 2, 0)
    out.cross(0)
    out.cross(1)
    back.hops(0, 2, 0)
    back.hops(0, 1, 1)
    back.hops(1, 1, 1)
    back.hops(1, 1, 0)
    back.hops(0, 1, 0)
    back.cross(0)
    back.cross(1)
    store_in_grad()
    out.rows(0)
    out.rows(1)
    out.across()
    back.rows(0)
    back.rows(1)
    back.across()
    mixed()
    finish()

    for copy in pending:
        copy.wait_send()
    store_out.wait()
    store_in.wait()


def local(block_in, norm_gain, weight_in, weight_out, output_grad):
    vmem, hbm = pl.BlockSpec(memory_space=pltpu.VMEM), pl.BlockSpec(memory_space=pl.ANY)
    rows, width = block_in.shape
    half = 2 * UNITS

    def buf(*shape, dtype=BF16):
        return pltpu.VMEM(shape, dtype)

    quarter = BLOCK // NX
    scratch = dict(
        wi=buf(WIDE, UNITS), wo=buf(UNITS, WIDE), std=buf(rows, width, dtype=F32),
        msg=buf(NX, 2 * ROWS, WIDE), got=buf(NX, 2 * ROWS, WIDE),
        acts=buf(2, 32, HALF, WIDE), cots=buf(2, 32, HALF, WIDE),
        terms=buf(2, 4, NX, quarter, UNITS), terms_in=buf(2, 4, NX - 1, quarter, UNITS),
        slope=buf(4, quarter, UNITS, dtype=F32),
        hid=buf(4, NX, quarter, UNITS), dpre=buf(4, NX, quarter, UNITS),
        hid_t=buf(UNITS, 4 * BLOCK), dpre_t=buf(UNITS, 4 * BLOCK),
        prod=buf(2, 2, 4, 2 * PER, HALF, WIDE), prod_sib=buf(2, 4, 2 * PER, HALF, WIDE),
        ring_in=buf(2, 2, 2, 4, 2, HALF, WIDE), ring_out=buf(2, 2, 2, 4, 2, HALF, WIDE),
        y_out=buf(2, 2, HALF, WIDE), y_in=buf(2, 2, HALF, WIDE),
        rows_out=buf(2, NX, ROWS, WIDE, dtype=F32), rows_in=buf(2, NX, ROWS, WIDE, dtype=F32),
        gsum=buf(2, 2, UNITS, half, dtype=F32), gsend=buf(2, UNITS, half),
        gin_got=buf(2, UNITS, half), gres=buf(UNITS, half, dtype=F32),
        gturn=buf(half, UNITS, dtype=F32),
        ssem=pltpu.SemaphoreType.DMA((SEMS,)), rsem=pltpu.SemaphoreType.DMA((SEMS,)),
        lsem=pltpu.SemaphoreType.DMA((4,)),
    )
    return pl.pallas_call(
        kernel,
        name="block",
        out_shape=(
            jax.ShapeDtypeStruct((rows, width), BF16),
            jax.ShapeDtypeStruct((rows, width), BF16),
            jax.ShapeDtypeStruct((half, UNITS), F32),
            jax.ShapeDtypeStruct((UNITS, half), F32),
        ),
        in_specs=[vmem, vmem, hbm, hbm, vmem],
        out_specs=(vmem, vmem, hbm, hbm),
        scratch_shapes=list(scratch.values()),
        compiler_params=pltpu.CompilerParams(
            collective_id=0, has_side_effects=True, vmem_limit_bytes=58 * 2**20
        ),
    )(block_in, norm_gain.reshape(1, width), weight_in, weight_out, output_grad)


def solution(mesh):
    in_specs = (P(("dp", "mp"), None), P(), P(None, "mp"), P("mp", None), P(("dp", "mp"), None))
    out_specs = (P(("dp", "mp"), None), P(("dp", "mp"), None), P("dp", "mp"), P("mp", "dp"))
    return jax.shard_map(local, mesh=mesh, in_specs=in_specs, out_specs=out_specs, check_vma=False)
```

```python
import jax
import jax.numpy as jnp
from jax import lax
from jax.experimental import pallas as pl
from jax.experimental.pallas import tpu as pltpu
from jax.sharding import PartitionSpec as P

MESH = pl.DeviceIdType.MESH
F32, BF16 = jnp.float32, jnp.bfloat16

NX, NZ = 4, 8
ROWS = 8
CHUNK = NX * ROWS
WIDE = 1536
UNITS = 384
BLOCK = 256
HALF = CHUNK // 2
PER = BLOCK // (4 * HALF)
FAR = 3
SEMS = 320
VMEM_ASKED = 60 * 2**20


def place():
    dp, mp = lax.axis_index("dp"), lax.axis_index("mp")
    return (
        lax.div(dp, 2),
        lax.rem(dp, 2),
        lax.div(mp, 16),
        lax.rem(lax.div(mp, 2), NZ),
        lax.rem(mp, 2),
    )


def device(x, yl, yh, z, c):
    return (x * 2 + yl, (yh * NZ + z) * 2 + c)


def slot(way, dist):
    if dist == 0:
        return 0
    if dist == 4:
        return 7
    return 2 * dist - 1 + way


def dot(left, right, dims=((1,), (0,))):
    return lax.dot_general(left, right, (dims, ((), ())), preferred_element_type=F32)


def standardise(x_ref):
    values = x_ref[...].astype(F32)
    average = jnp.mean(values, axis=1, keepdims=True)
    centred = values - average
    inv_scale = lax.rsqrt(jnp.mean(centred * centred, axis=1, keepdims=True) + 1e-06)
    return centred * inv_scale, inv_scale


def finish_kernel(
    x_any, gain_any, g_any, rows_any, gin_any, gout_any,
    mixed_any, igrad_any, gin_out, gout_out,
    x_ref, gain_ref, g_ref, rows, gin, turned, gout, mixed, igrad, sems, osems,
):
    pairs = (
        (gin_any, gin), (x_any, x_ref), (gain_any, gain_ref), (g_any, g_ref), (rows_any, rows),
        (gout_any, gout))
    loads = [pltpu.make_async_copy(a, b, sems.at[k]) for k, (a, b) in enumerate(pairs)]
    for copy in loads:
        copy.start()
    stores = [
        pltpu.make_async_copy(a, b, osems.at[k])
        for k, (a, b) in enumerate((
            (turned, gin_out), (mixed, mixed_any), (igrad, igrad_any), (gout, gout_out)))]
    loads[0].wait()
    turned[...] = gin[...].T
    stores[0].start()
    for copy in loads[1:]:
        copy.wait()
    stores[3].start()
    width = x_ref.shape[1]
    for a in range(NX):
        cols = slice(a * WIDE, (a + 1) * WIDE)
        mixed[:, cols] = (x_ref[:, cols].astype(F32) + rows[0, a]).astype(BF16)
    stores[1].start()
    standard, inv_scale = standardise(x_ref)
    scaled = [rows[1, a] * gain_ref[:, a * WIDE:(a + 1) * WIDE] for a in range(NX)]
    standards = [standard[:, a * WIDE:(a + 1) * WIDE] for a in range(NX)]
    mean_scaled = sum(jnp.sum(s, axis=1, keepdims=True) for s in scaled) / width
    mean_both = sum(
        jnp.sum(s * t, axis=1, keepdims=True) for s, t in zip(scaled, standards)) / width
    for a in range(NX):
        cols = slice(a * WIDE, (a + 1) * WIDE)
        change = inv_scale * (scaled[a] - mean_scaled - standards[a] * mean_both)
        igrad[:, cols] = (g_ref[:, cols].astype(F32) + change).astype(BF16)
    stores[2].start()
    for copy in stores:
        copy.wait()


def kernel(
    x_any, gain_any, wi_any, wo_any, g_any,
    rows_any, gin_any, gout_any,
    x_ref, gain_ref, g_ref, wi, wo, msg, got, acts, cots,
    terms, terms_in, slope, hid, dpre, hid_t, dpre_t,
    prod, prod_sib, ring_in, ring_out, y_out, y_in, rows_out, rows_in,
    gsum, gsend, gin_got, gres,
    ssem, rsem, lsem,
):
    x, yl, yh, z, c = place()
    xs = [lax.rem(x + k, NX) for k in range(NX)]
    zp, zm = lax.rem(z + 1, NZ), lax.rem(z + NZ - 1, NZ)
    to_z = (device(x, yl, yh, zp, c), device(x, yl, yh, zm, c))
    to_sib = device(x, yl, yh, z, 1 - c)
    to_yh = device(x, yl, 1 - yh, z, c)
    to_yl = device(x, 1 - yl, yh, z, c)
    to_x = [device(xs[k], yl, yh, z, c) for k in range(NX)]

    barrier = pltpu.get_barrier_semaphore()
    for other in (*to_z, to_sib, to_yh, to_yl, *to_x[1:]):
        pl.semaphore_signal(barrier, inc=1, device_id=other, device_id_type=MESH)

    load_wi = pltpu.make_async_copy(
        wi_any.at[pl.ds(pl.multiple_of(x * WIDE, WIDE), WIDE)], wi, lsem.at[0])
    load_wo = pltpu.make_async_copy(
        wo_any.at[:, pl.ds(pl.multiple_of(x * WIDE, WIDE), WIDE)], wo, lsem.at[1])
    loads = [
        pltpu.make_async_copy(src, dst, lsem.at[4 + k])
        for k, (src, dst) in enumerate(((x_any, x_ref), (gain_any, gain_ref), (g_any, g_ref)))]
    for copy in loads:
        copy.start()
    load_wi.start()
    load_wo.start()
    for copy in loads:
        copy.wait()

    normed = standardise(x_ref)[0] * gain_ref[...]
    grad = g_ref[...].astype(F32)
    for q in range(NX):
        cols = slice(q * WIDE, (q + 1) * WIDE)
        msg[q] = jnp.concatenate([normed[:, cols], grad[:, cols]], axis=0).astype(BF16)

    pl.semaphore_wait(barrier, 8)

    pending = []

    def send(src, dst, to):
        k = len(pending)
        copy = pltpu.make_async_remote_copy(
            src_ref=src, dst_ref=dst, send_sem=ssem.at[k], recv_sem=rsem.at[k],
            device_id=to, device_id_type=MESH)
        copy.start()
        pending.append(copy)
        return copy

    first = [send(msg.at[xs[k]], got.at[x], to_x[k]) for k in range(1, NX)]
    got[x] = msg[x]
    for copy in first:
        copy.wait_recv()
    pieces = [got[a].astype(F32) for a in range(NX)]
    for part in (0, 1):
        pair = pieces[2 * part:2 * part + 2]
        acts[part, 0] = jnp.concatenate([p[:ROWS] for p in pair], axis=0).astype(BF16)
        cots[part, 0] = jnp.concatenate([p[ROWS:] for p in pair], axis=0).astype(BF16)

    def ways(dist, part, turn):
        return (0, 1) if dist < 4 else (part ^ turn,)

    class Gather:
        def __init__(self, buf, turn):
            self.buf, self.turn = buf, turn
            self.near, self.ring, self.y, self.sib = {}, {}, {}, {}

        def at(self, part, s, h):
            return self.buf.at[part, 4 * s + h]

        def pass_on(self, part, way, dist, h):
            here = self.at(part, slot(way, dist), h)
            if dist < (FAR - 1 if h else 4) and way in ways(dist + 1, part, self.turn):
                there = self.at(part, slot(way, dist + 1), h)
                self.ring[part, way, dist + 1, h] = send(here, there, to_z[way])
            if dist >= FAR and h == 0:
                there = self.at(part, slot(way, dist), 1)
                self.y[part, way, dist] = send(here, there, to_yh)

        def to_core(self, part, s):
            self.sib[part, s] = send(
                self.buf.at[part, pl.ds(4 * s, 2)], self.buf.at[part, pl.ds(4 * s + 2, 2)], to_sib)

        def start(self, part):
            self.near[part] = send(self.at(part, 0, 0), self.at(part, 0, 1), to_yh)
            for way in (0, 1):
                self.pass_on(part, way, 0, 0)

        def other(self, part):
            self.near[part].wait_recv()
            for way in (0, 1):
                self.pass_on(part, way, 0, 1)
            self.to_core(part, 0)

        def own(self, part, dist):
            for way in ways(dist, part, self.turn):
                self.ring[part, way, dist, 0].wait_recv()
                self.pass_on(part, way, dist, 0)

        def oth(self, part, dist):
            for way in (0, 1):
                self.ring[part, way, dist, 1].wait_recv()
                self.pass_on(part, way, dist, 1)
                self.to_core(part, slot(way, dist))

        def far(self, part, dist):
            for way in ways(dist, part, self.turn):
                self.y[part, way, dist].wait_recv()
                self.to_core(part, slot(way, dist))

        def block(self, part, b):
            for s in range(PER * b, PER * b + PER):
                self.sib[part, s].wait_recv()
            return self.buf[part, 4 * PER * b:4 * PER * (b + 1)].reshape(BLOCK, WIDE)

    class Across:
        def __init__(self, i, result):
            self.term, self.came, self.result = terms.at[i], terms_in.at[i], result
            self.out, self.back = {}, {}

        def give(self, b, term):
            self.term[b] = term.astype(BF16).reshape(NX, BLOCK // NX, UNITS)
            self.out[b] = [
                send(self.term.at[b, xs[k]], self.came.at[b, k - 1], to_x[k]) for k in range(1, NX)]

        def total(self, b):
            for copy in self.out[b]:
                copy.wait_recv()
            total = self.term[b, x].astype(F32)
            for k in range(NX - 1):
                total = total + self.came[b, k].astype(F32)
            return total

        def share(self, b, value):
            self.result[b, x] = value.astype(BF16)
            self.back[b] = [
                send(self.result.at[b, x], self.result.at[b, x], to_x[k]) for k in range(1, NX)]

        def whole(self, b):
            for copy in self.back[b]:
                copy.wait_recv()
            return self.result[b].reshape(BLOCK, UNITS)

    class Scatter:
        def __init__(self, i, turn):
            self.turn = turn
            self.prod, self.sib = prod.at[i], prod_sib.at[i]
            self.rin, self.rout = ring_in.at[i], ring_out.at[i]
            self.yout, self.yin = y_out.at[i], y_in.at[i]
            self.xout, self.xin = rows_out.at[i], rows_in.at[i]
            self.sibs, self.ring, self.y, self.seen = {}, {}, {}, set()

        def give(self, k, left, right, dims):
            for n in range(0, WIDE, 512):
                if dims == 1:
                    term = dot(left, right[n:n + 512, :], ((1,), (1,)))
                else:
                    term = dot(left, right[:, n:n + 512])
                term = term.astype(BF16).reshape(PER, 2, 2, HALF, 512)
                for core in (0, 1):
                    self.prod[core, k, :, :, n:n + 512] = term[:, core].reshape(2 * PER, HALF, 512)
            self.sibs[k] = send(self.prod.at[1, k], self.sib.at[k], to_sib)

        def term(self, part, s, h):
            k, q = 2 * part + s // PER, 2 * (s % PER) + h
            if k not in self.seen:
                self.seen.add(k)
                self.sibs[k].wait_recv()
            return self.prod[0, k, q].astype(F32) + self.sib[k, q].astype(F32)

        def hop(self, part, way, dist, h):
            value = self.term(part, slot(way, dist), h)
            if (part, way, dist, h) in self.ring:
                self.ring[part, way, dist, h].wait_recv()
                value = value + self.rin[part, way, dist, h].astype(F32)
            self.rout[part, way, dist - 1, h] = value.astype(BF16)
            self.ring[part, way, dist - 1, h] = send(
                self.rout.at[part, way, dist - 1, h], self.rin.at[part, way, dist - 1, h],
                to_z[1 - way])

        def hops(self, part, dist, h):
            for way in ways(dist, part, self.turn):
                self.hop(part, way, dist, h)

        def near(self, part, h):
            value = self.term(part, 0, h)
            for way in (0, 1):
                self.ring[part, way, 0, h].wait_recv()
                value = value + self.rin[part, way, 0, h].astype(F32)
            return value

        def cross(self, part):
            self.yout[part] = self.near(part, 1).astype(BF16)
            self.y[part] = send(self.yout.at[part], self.yin.at[part], to_yh)

        def rows(self, part):
            value = self.near(part, 0)
            self.y[part].wait_recv()
            value = value + self.yin[part].astype(F32)
            self.xout[2 * part:2 * part + 2] = value.reshape(2, ROWS, WIDE)

        def across(self):
            self.x = [send(self.xout.at[xs[k]], self.xin.at[x], to_x[k]) for k in range(1, NX)]
            self.xin[x] = self.xout[x]

        def done(self):
            for copy in self.x:
                copy.wait_recv()

    class Weights:
        def __init__(self, i):
            self.sum, self.out, self.came = gsum.at[i], gsend.at[i], gin_got.at[i]

        def give(self, left_t, right):
            left = left_t[...]
            for n in range(4):
                cols = slice(n * UNITS, (n + 1) * UNITS)
                term = dot(left, right[:, :, :, cols].reshape(4 * BLOCK, UNITS))
                self.sum[n // 2, :, (n % 2) * UNITS:(n % 2 + 1) * UNITS] = term
            self.out[...] = self.sum[1 - yl].astype(BF16)
            self.copy = send(self.out, self.came, to_yl)

        def total(self):
            self.copy.wait_recv()
            return self.sum[yl] + self.came[...].astype(F32)

    ga, gg = Gather(acts, 0), Gather(cots, 1)
    fwd, bwd = Across(0, hid), Across(1, dpre)
    out, back = Scatter(0, 0), Scatter(1, 1)
    w_out, w_in = Weights(0), Weights(1)

    def pre(part, b):
        fwd.give(2 * part + b, dot(ga.block(part, b), wi[...]))

    def act(part, b):
        k = 2 * part + b
        value = fwd.total(k)
        cdf = 0.5 * (1.0 + lax.erf(value * 0.7071067811865476))
        slope[k] = cdf + value * jnp.exp(-0.5 * value * value) * 0.3989422804014327
        fwd.share(k, value * cdf)

    def cot(part, b):
        bwd.give(2 * part + b, dot(gg.block(part, b), wo[...], ((1,), (1,))))

    def act_back(part, b):
        k = 2 * part + b
        bwd.share(k, bwd.total(k) * slope[k])

    def branch(part, b):
        k = 2 * part + b
        value = fwd.whole(k)
        hid_t[:, k * BLOCK:(k + 1) * BLOCK] = value.T
        out.give(k, value, wo, 0)

    def back_prod(part, b):
        k = 2 * part + b
        value = bwd.whole(k)
        dpre_t[:, k * BLOCK:(k + 1) * BLOCK] = value.T
        back.give(k, value, wi, 1)

    def mixed():
        out.done()
        keep_out.start()

    def store_out_grad():
        gres[0] = w_out.total()
        store_out.start()

    def store_in_grad():
        gres[1] = w_in.total()
        store_in.start()

    def finish():
        back.done()
        keep_back.start()

    store_out = pltpu.make_async_copy(gres.at[0], gout_any, lsem.at[2])
    store_in = pltpu.make_async_copy(gres.at[1], gin_any, lsem.at[3])
    keep_out = pltpu.make_async_copy(rows_in.at[0], rows_any.at[0], lsem.at[7])
    keep_back = pltpu.make_async_copy(rows_in.at[1], rows_any.at[1], lsem.at[8])

    ga.start(0)
    ga.start(1)
    ga.own(0, 1)
    ga.other(0)
    ga.own(1, 1)
    ga.other(1)
    ga.own(0, 2)
    ga.oth(0, 1)
    gg.start(0)
    ga.own(1, 2)
    gg.start(1)
    ga.oth(1, 1)
    ga.own(0, 3)
    ga.oth(0, 2)
    load_wi.wait()
    load_wo.wait()
    pre(0, 0)
    gg.other(0)
    gg.own(0, 1)
    ga.own(1, 3)
    gg.other(1)
    gg.own(1, 1)
    ga.far(0, 3)
    ga.oth(1, 2)
    ga.own(0, 4)
    gg.oth(0, 1)
    act(0, 0)
    ga.far(1, 3)
    gg.own(0, 2)
    pre(1, 0)
    ga.own(1, 4)
    gg.oth(1, 1)
    ga.far(0, 4)
    gg.own(1, 2)
    pre(0, 1)
    branch(0, 0)
    ga.far(1, 4)
    act(1, 0)
    gg.own(0, 3)
    gg.oth(1, 2)
    gg.own(1, 3)
    pre(1, 1)
    cot(1, 0)
    gg.own(0, 4)
    gg.own(1, 4)
    branch(1, 0)
    gg.far(0, 3)
    act(0, 1)
    gg.oth(0, 2)
    act(1, 1)
    gg.far(1, 3)
    cot(0, 0)
    act_back(1, 0)
    gg.far(1, 4)
    gg.far(0, 4)
    branch(0, 1)
    cot(0, 1)
    cot(1, 1)
    branch(1, 1)
    w_out.give(hid_t, cots)
    out.hops(1, 4, 1)
    out.hops(1, 4, 0)
    out.hops(0, 4, 0)
    out.hops(0, 4, 1)
    act_back(0, 0)
    back_prod(1, 0)
    act_back(0, 1)
    out.hops(0, 3, 0)
    act_back(1, 1)
    out.hops(0, 3, 1)
    out.hops(1, 3, 1)
    out.hops(1, 3, 0)
    back_prod(0, 0)
    out.hops(0, 2, 0)
    back_prod(0, 1)
    out.hops(0, 2, 1)
    out.hops(1, 2, 1)
    back_prod(1, 1)
    back.hops(0, 4, 1)
    back.hops(0, 4, 0)
    out.hops(0, 1, 0)
    out.hops(0, 1, 1)
    back.hops(1, 4, 1)
    out.hops(1, 2, 0)
    out.hops(1, 1, 1)
    back.hops(1, 4, 0)
    w_in.give(dpre_t, acts)
    back.hops(0, 3, 0)
    back.hops(0, 3, 1)
    store_out_grad()
    back.hops(1, 3, 1)
    back.hops(1, 3, 0)
    out.hops(1, 1, 0)
    back.hops(0, 2, 1)
    back.hops(1, 2, 1)
    back.hops(1, 2, 0)
    out.cross(0)
    out.cross(1)
    back.hops(0, 2, 0)
    back.hops(0, 1, 1)
    back.hops(1, 1, 1)
    back.hops(1, 1, 0)
    back.hops(0, 1, 0)
    back.cross(0)
    back.cross(1)
    store_in_grad()
    out.rows(0)
    out.rows(1)
    out.across()
    back.rows(0)
    back.rows(1)
    back.across()
    mixed()
    finish()

    for copy in pending:
        copy.wait_send()
    for copy in (store_out, store_in, keep_out, keep_back):
        copy.wait()


def local(block_in, norm_gain, weight_in, weight_out, output_grad):
    hbm = pl.BlockSpec(memory_space=pl.ANY)
    rows, width = block_in.shape
    half = 2 * UNITS
    gain = norm_gain.reshape(1, width)

    def buf(*shape, dtype=BF16):
        return pltpu.VMEM(shape, dtype)

    quarter = BLOCK // NX
    inputs = dict(x=buf(rows, width), gain=buf(1, width, dtype=F32), g=buf(rows, width))
    scratch = dict(
        **inputs, wi=buf(WIDE, UNITS), wo=buf(UNITS, WIDE),
        msg=buf(NX, 2 * ROWS, WIDE), got=buf(NX, 2 * ROWS, WIDE),
        acts=buf(2, 32, HALF, WIDE), cots=buf(2, 32, HALF, WIDE),
        terms=buf(2, 4, NX, quarter, UNITS), terms_in=buf(2, 4, NX - 1, quarter, UNITS),
        slope=buf(4, quarter, UNITS, dtype=F32),
        hid=buf(4, NX, quarter, UNITS), dpre=buf(4, NX, quarter, UNITS),
        hid_t=buf(UNITS, 4 * BLOCK), dpre_t=buf(UNITS, 4 * BLOCK),
        prod=buf(2, 2, 4, 2 * PER, HALF, WIDE), prod_sib=buf(2, 4, 2 * PER, HALF, WIDE),
        ring_in=buf(2, 2, 2, 4, 2, HALF, WIDE), ring_out=buf(2, 2, 2, 4, 2, HALF, WIDE),
        y_out=buf(2, 2, HALF, WIDE), y_in=buf(2, 2, HALF, WIDE),
        rows_out=buf(2, NX, ROWS, WIDE, dtype=F32), rows_in=buf(2, NX, ROWS, WIDE, dtype=F32),
        gsum=buf(2, 2, UNITS, half, dtype=F32), gsend=buf(2, UNITS, half),
        gin_got=buf(2, UNITS, half), gres=buf(2, UNITS, half, dtype=F32),
        ssem=pltpu.SemaphoreType.DMA((SEMS,)), rsem=pltpu.SemaphoreType.DMA((SEMS,)),
        lsem=pltpu.SemaphoreType.DMA((9,)),
    )
    summed, gin_t, gout = pl.pallas_call(
        kernel,
        name="block",
        out_shape=(
            jax.ShapeDtypeStruct((2, NX, rows, WIDE), F32),
            jax.ShapeDtypeStruct((UNITS, half), F32),
            jax.ShapeDtypeStruct((UNITS, half), F32),
        ),
        in_specs=[hbm] * 5,
        out_specs=(hbm,) * 3,
        scratch_shapes=list(scratch.values()),
        compiler_params=pltpu.CompilerParams(
            collective_id=0, has_side_effects=True, vmem_limit_bytes=VMEM_ASKED
        ),
    )(block_in, gain, weight_in, weight_out, output_grad)
    return pl.pallas_call(
        finish_kernel,
        name="finish",
        out_shape=(
            jax.ShapeDtypeStruct((rows, width), BF16),
            jax.ShapeDtypeStruct((rows, width), BF16),
            jax.ShapeDtypeStruct((half, UNITS), F32),
            jax.ShapeDtypeStruct((UNITS, half), F32),
        ),
        in_specs=[hbm] * 6,
        out_specs=(hbm,) * 4,
        scratch_shapes=[
            *inputs.values(), buf(2, NX, rows, WIDE, dtype=F32), buf(UNITS, half, dtype=F32),
            buf(half, UNITS, dtype=F32), buf(UNITS, half, dtype=F32), buf(rows, width),
            buf(rows, width), pltpu.SemaphoreType.DMA((6,)), pltpu.SemaphoreType.DMA((4,)),
        ],
        compiler_params=pltpu.CompilerParams(vmem_limit_bytes=VMEM_ASKED),
    )(block_in, gain, output_grad, summed, gin_t, gout)


def solution(mesh):
    in_specs = (P(("dp", "mp"), None), P(), P(None, "mp"), P("mp", None), P(("dp", "mp"), None))
    out_specs = (P(("dp", "mp"), None), P(("dp", "mp"), None), P("dp", "mp"), P("mp", "dp"))
    return jax.shard_map(local, mesh=mesh, in_specs=in_specs, out_specs=out_specs, check_vma=False)
```

```python
import jax
import jax.numpy as jnp
from jax import lax
from jax.experimental import pallas as pl
from jax.experimental.pallas import tpu as pltpu
from jax.sharding import PartitionSpec as P

MESH = pl.DeviceIdType.MESH
F32, BF16 = jnp.float32, jnp.bfloat16

NX, NZ = 4, 8
ROWS = 8
CHUNK = NX * ROWS
WIDE = 1536
UNITS = 384
BLOCK = 256
SIDE = WIDE // 2
UNIT = 2 * ROWS
PER = BLOCK // (4 * CHUNK)
FAR = 4
SEMS = 320
VMEM_ASKED = 60 * 2**20


def place():
    dp, mp = lax.axis_index("dp"), lax.axis_index("mp")
    return (
        lax.div(dp, 2),
        lax.rem(dp, 2),
        lax.div(mp, 16),
        lax.rem(lax.div(mp, 2), NZ),
        lax.rem(mp, 2),
    )


def device(x, yl, yh, z, c):
    return (x * 2 + yl, (yh * NZ + z) * 2 + c)


def slot(way, dist):
    if dist == 0:
        return 0
    if dist == 4:
        return 7
    return 2 * dist - 1 + way


def dot(left, right, dims=((1,), (0,))):
    return lax.dot_general(left, right, (dims, ((), ())), preferred_element_type=F32)


def standardise(x_ref):
    values = x_ref[...].astype(F32)
    average = jnp.mean(values, axis=1, keepdims=True)
    centred = values - average
    inv_scale = lax.rsqrt(jnp.mean(centred * centred, axis=1, keepdims=True) + 1e-06)
    return centred * inv_scale, inv_scale


def finish_kernel(
    x_any, gain_any, g_any, rows_any, gin_any, gout_any,
    mixed_any, igrad_any, gin_out, gout_out,
    x_ref, gain_ref, g_ref, rows, gin, turned, gout, mixed, igrad, sems, osems,
):
    pairs = (
        (gin_any, gin), (x_any, x_ref), (gain_any, gain_ref), (g_any, g_ref), (rows_any, rows),
        (gout_any, gout))
    loads = [pltpu.make_async_copy(a, b, sems.at[k]) for k, (a, b) in enumerate(pairs)]
    for copy in loads:
        copy.start()
    stores = [
        pltpu.make_async_copy(a, b, osems.at[k])
        for k, (a, b) in enumerate((
            (turned, gin_out), (mixed, mixed_any), (igrad, igrad_any), (gout, gout_out)))]
    loads[0].wait()
    turned[...] = gin[...].T
    stores[0].start()
    for copy in loads[1:]:
        copy.wait()
    stores[3].start()
    width = x_ref.shape[1]
    for a in range(NX):
        cols = slice(a * WIDE, (a + 1) * WIDE)
        mixed[:, cols] = (x_ref[:, cols].astype(F32) + rows[0, a]).astype(BF16)
    stores[1].start()
    standard, inv_scale = standardise(x_ref)
    scaled = [rows[1, a] * gain_ref[:, a * WIDE:(a + 1) * WIDE] for a in range(NX)]
    standards = [standard[:, a * WIDE:(a + 1) * WIDE] for a in range(NX)]
    mean_scaled = sum(jnp.sum(s, axis=1, keepdims=True) for s in scaled) / width
    mean_both = sum(
        jnp.sum(s * t, axis=1, keepdims=True) for s, t in zip(scaled, standards)) / width
    for a in range(NX):
        cols = slice(a * WIDE, (a + 1) * WIDE)
        change = inv_scale * (scaled[a] - mean_scaled - standards[a] * mean_both)
        igrad[:, cols] = (g_ref[:, cols].astype(F32) + change).astype(BF16)
    stores[2].start()
    for copy in stores:
        copy.wait()


def kernel(
    x_any, gain_any, wi_any, wo_any, g_any,
    rows_any, gin_any, gout_any,
    x_ref, gain_ref, g_ref, wi, wo, msg, got, acts, cots,
    terms, terms_in, slope, hid, dpre, hid_t, dpre_t,
    prod, prod_sib, ring_in, ring_out, y_out, y_in, rows_out,
    gsum, gsend, gin_got, gres,
    ssem, rsem, lsem, ksem,
):
    x, yl, yh, z, c = place()
    xs = [lax.rem(x + k, NX) for k in range(NX)]
    zp, zm = lax.rem(z + 1, NZ), lax.rem(z + NZ - 1, NZ)
    to_z = (device(x, yl, yh, zp, c), device(x, yl, yh, zm, c))
    to_sib = device(x, yl, yh, z, 1 - c)
    to_yh = device(x, yl, 1 - yh, z, c)
    to_yl = device(x, 1 - yl, yh, z, c)
    to_x = [device(xs[k], yl, yh, z, c) for k in range(NX)]

    barrier = pltpu.get_barrier_semaphore()
    for other in (*to_z, to_sib, to_yh, to_yl, *to_x[1:]):
        pl.semaphore_signal(barrier, inc=1, device_id=other, device_id_type=MESH)

    weights = []
    for a in range(NX):
        cols = pl.ds(a * WIDE, WIDE)
        weights.append(pltpu.make_async_copy(wi_any.at[cols], wi.at[a], lsem.at[5 + a]))
        weights.append(pltpu.make_async_copy(wo_any.at[:, cols], wo.at[a], lsem.at[9 + a]))

    loads = [
        pltpu.make_async_copy(src, dst, lsem.at[2 + k])
        for k, (src, dst) in enumerate(((x_any, x_ref), (gain_any, gain_ref), (g_any, g_ref)))]
    for copy in loads:
        copy.start()
    for copy in weights:
        copy.start()
    for copy in loads:
        copy.wait()

    normed = standardise(x_ref)[0] * gain_ref[...]
    grad = g_ref[...].astype(F32)
    for q in range(NX):
        cols = slice(q * WIDE, (q + 1) * WIDE)
        msg[q] = jnp.concatenate([normed[:, cols], grad[:, cols]], axis=0).astype(BF16)

    pl.semaphore_wait(barrier, 8)

    pending = []

    def send(src, dst, to):
        k = len(pending)
        copy = pltpu.make_async_remote_copy(
            src_ref=src, dst_ref=dst, send_sem=ssem.at[k], recv_sem=rsem.at[k],
            device_id=to, device_id_type=MESH)
        copy.start()
        pending.append(copy)
        return copy

    first = [send(msg.at[xs[k]], got.at[x], to_x[k]) for k in range(1, NX)]
    got[x] = msg[x]
    for copy in first:
        copy.wait_recv()
    pieces = [got[a].astype(F32) for a in range(NX)]
    for part in (0, 1):
        cols = slice(part * SIDE, (part + 1) * SIDE)
        acts[part, 0] = jnp.concatenate([p[:ROWS, cols] for p in pieces], axis=0).astype(BF16)
        cots[part, 0] = jnp.concatenate([p[ROWS:, cols] for p in pieces], axis=0).astype(BF16)

    def ways(dist, part, turn):
        return (0, 1) if dist < 4 else (part ^ turn,)

    class Gather:
        def __init__(self, buf, turn):
            self.buf, self.turn = buf, turn
            self.near, self.ring, self.y, self.sib = {}, {}, {}, {}

        def at(self, part, s, h):
            return self.buf.at[part, 4 * s + h]

        def pass_on(self, part, way, dist, h):
            here = self.at(part, slot(way, dist), h)
            if dist < (FAR - 1 if h else 4) and way in ways(dist + 1, part, self.turn):
                there = self.at(part, slot(way, dist + 1), h)
                self.ring[part, way, dist + 1, h] = send(here, there, to_z[way])
            if dist >= FAR and h == 0:
                there = self.at(part, slot(way, dist), 1)
                self.y[part, way, dist] = send(here, there, to_yh)

        def to_core(self, part, s):
            self.sib[part, s] = send(
                self.buf.at[part, pl.ds(4 * s, 2)], self.buf.at[part, pl.ds(4 * s + 2, 2)], to_sib)

        def start(self, part):
            self.near[part] = send(self.at(part, 0, 0), self.at(part, 0, 1), to_yh)
            for way in (0, 1):
                self.pass_on(part, way, 0, 0)

        def other(self, part):
            self.near[part].wait_recv()
            for way in (0, 1):
                self.pass_on(part, way, 0, 1)
            self.to_core(part, 0)

        def own(self, part, dist):
            for way in ways(dist, part, self.turn):
                self.ring[part, way, dist, 0].wait_recv()
                self.pass_on(part, way, dist, 0)

        def oth(self, part, dist):
            for way in (0, 1):
                self.ring[part, way, dist, 1].wait_recv()
                self.pass_on(part, way, dist, 1)
                self.to_core(part, slot(way, dist))

        def far(self, part, dist):
            for way in ways(dist, part, self.turn):
                self.y[part, way, dist].wait_recv()
                self.to_core(part, slot(way, dist))

        def block(self, b):
            for s in range(PER * b, PER * b + PER):
                for part in (0, 1):
                    self.sib[part, s].wait_recv()
            return [
                self.buf[part, 8 * b:8 * b + 8].reshape(BLOCK, SIDE) for part in (0, 1)]

    class Across:
        def __init__(self, i, result):
            self.term, self.came, self.result = terms.at[i], terms_in.at[i], result
            self.out, self.back = {}, {}

        def give(self, b, term):
            term = term.reshape(8, NX, ROWS, UNITS)
            for q in range(NX):
                self.term[b, q] = term[:, q].reshape(8 * ROWS, UNITS).astype(BF16)
            self.out[b] = [
                send(self.term.at[b, xs[k]], self.came.at[b, k - 1], to_x[k]) for k in range(1, NX)]

        def total(self, b):
            for copy in self.out[b]:
                copy.wait_recv()
            total = self.term[b, x].astype(F32)
            for k in range(NX - 1):
                total = total + self.came[b, k].astype(F32)
            return total

        def share(self, b, value):
            self.result[b, x] = value.astype(BF16)
            self.back[b] = [
                send(self.result.at[b, x], self.result.at[b, x], to_x[k]) for k in range(1, NX)]

        def own(self):
            return self.result[:, x].reshape(BLOCK, UNITS)

        def turned(self, b):
            for copy in self.back[b]:
                copy.wait_recv()
            value = self.result[b].astype(F32).reshape(NX, 8, ROWS, UNITS)
            rows = [value[q, k] for k in range(8) for q in range(NX)]
            return jnp.concatenate(rows, axis=0).T.astype(BF16)

    class Scatter:
        def __init__(self, i, turn):
            self.turn = turn
            self.prod, self.sib = prod.at[i], prod_sib.at[i]
            self.rin, self.rout = ring_in.at[i], ring_out.at[i]
            self.yout, self.yin = y_out.at[i], y_in.at[i]
            self.rows_out, self.rows_hbm = rows_out.at[i], rows_any.at[i]
            self.sibs, self.ring, self.y, self.seen = {}, {}, {}, set()
            self.keep, self.keep_sem = {}, ksem.at[i]

        def give(self, part, left, right, turned):
            for n in range(0, WIDE, 512):
                pair = []
                for a in (2 * part, 2 * part + 1):
                    if turned:
                        term = dot(left, right[a, n:n + 512, :], ((1,), (1,)))
                    else:
                        term = dot(left, right[a, :, n:n + 512])
                    pair.append(term.reshape(NZ, 2, 2, ROWS, 512))
                term = jnp.concatenate(pair, axis=3).astype(BF16)
                for core in (0, 1):
                    rows = term[:, core].reshape(2 * NZ, UNIT, 512)
                    self.prod[core, part, :, :, n:n + 512] = rows
            for k in (1, 0):
                rows = pl.ds(NZ * k, NZ)
                self.sibs[part, k] = send(
                    self.prod.at[1, part, rows], self.sib.at[part, rows], to_sib)

        def term(self, part, s, h):
            k, q = s // 4, 2 * s + h
            if (part, k) not in self.seen:
                self.seen.add((part, k))
                self.sibs[part, k].wait_recv()
            return self.prod[0, part, q].astype(F32) + self.sib[part, q].astype(F32)

        def hop(self, part, way, dist, h):
            value = self.term(part, slot(way, dist), h)
            if (part, way, dist, h) in self.ring:
                self.ring[part, way, dist, h].wait_recv()
                value = value + self.rin[part, way, dist, h].astype(F32)
            self.rout[part, way, dist - 1, h] = value.astype(BF16)
            self.ring[part, way, dist - 1, h] = send(
                self.rout.at[part, way, dist - 1, h], self.rin.at[part, way, dist - 1, h],
                to_z[1 - way])

        def hops(self, part, dist, h):
            for way in ways(dist, part, self.turn):
                self.hop(part, way, dist, h)

        def near(self, part, h):
            value = self.term(part, 0, h)
            for way in (0, 1):
                self.ring[part, way, 0, h].wait_recv()
                value = value + self.rin[part, way, 0, h].astype(F32)
            return value

        def cross(self, part):
            self.yout[part] = self.near(part, 1).astype(BF16)
            self.y[part] = send(self.yout.at[part], self.yin.at[part], to_yh)

        def rows(self, part):
            value = self.near(part, 0)
            self.y[part].wait_recv()
            value = value + self.yin[part].astype(F32)
            self.rows_out[2 * part:2 * part + 2] = value.reshape(2, ROWS, WIDE)
            cols = pl.ds(2 * part, 2)
            self.keep[part] = pltpu.make_async_copy(
                self.rows_out.at[cols], self.rows_hbm.at[cols], self.keep_sem.at[part])
            self.keep[part].start()

    class Weights:
        def __init__(self, i):
            self.sum, self.out, self.came = gsum.at[i], gsend.at[i], gin_got.at[i]

        def give(self, left_t, right):
            left = left_t[...]
            for n in range(4):
                cols = slice((n % 2) * UNITS, (n % 2 + 1) * UNITS)
                term = dot(left, right[n // 2, :, :, cols].reshape(4 * BLOCK, UNITS))
                self.sum[n // 2, :, cols] = term
            self.out[...] = self.sum[1 - yl].astype(BF16)
            self.copy = send(self.out, self.came, to_yl)

        def total(self):
            self.copy.wait_recv()
            return self.sum[yl] + self.came[...].astype(F32)

    ga, gg = Gather(acts, 0), Gather(cots, 1)
    fwd, bwd = Across(0, hid), Across(1, dpre)
    out, back = Scatter(0, 0), Scatter(1, 1)
    w_out, w_in = Weights(0), Weights(1)

    def pre(b):
        sides = ga.block(b)
        fwd.give(b, dot(sides[0], wi[x, :SIDE]) + dot(sides[1], wi[x, SIDE:]))

    def act(b):
        value = fwd.total(b)
        cdf = 0.5 * (1.0 + lax.erf(value * 0.7071067811865476))
        slope[b] = cdf + value * jnp.exp(-0.5 * value * value) * 0.3989422804014327
        fwd.share(b, value * cdf)

    def cot(b):
        sides, dims = gg.block(b), ((1,), (1,))
        bwd.give(b, dot(sides[0], wo[x, :, :SIDE], dims) + dot(sides[1], wo[x, :, SIDE:], dims))

    def act_back(b):
        bwd.share(b, bwd.total(b) * slope[b])

    def branch(part):
        out.give(part, fwd.own(), wo, False)

    def back_prod(part):
        back.give(part, bwd.own(), wi, True)

    def turn(b):
        hid_t[:, b * BLOCK:(b + 1) * BLOCK] = fwd.turned(b)

    def turn_back(b):
        dpre_t[:, b * BLOCK:(b + 1) * BLOCK] = bwd.turned(b)

    def store_out_grad():
        gres[0] = w_out.total()
        store_out.start()

    def store_in_grad():
        gres[1] = w_in.total()
        store_in.start()

    store_out = pltpu.make_async_copy(gres.at[0], gout_any, lsem.at[0])
    store_in = pltpu.make_async_copy(gres.at[1], gin_any, lsem.at[1])

    ga.start(1)
    ga.start(0)
    ga.own(1, 1)
    ga.own(0, 1)
    ga.other(0)
    ga.other(1)
    ga.own(1, 2)
    ga.own(0, 2)
    ga.oth(0, 1)
    ga.oth(1, 1)
    ga.own(1, 3)
    ga.own(0, 3)
    gg.start(0)
    gg.start(1)
    for copy in weights:
        copy.wait()
    pre(0)
    ga.oth(0, 2)
    ga.oth(1, 2)
    pre(1)
    gg.own(0, 1)
    gg.other(1)
    ga.own(0, 4)
    ga.own(1, 4)
    gg.own(1, 1)
    gg.other(0)
    ga.oth(0, 3)
    act(0)
    ga.oth(1, 3)
    pre(2)
    gg.own(0, 2)
    ga.far(0, 4)
    gg.oth(1, 1)
    gg.own(1, 2)
    ga.far(1, 4)
    pre(3)
    gg.own(0, 3)
    gg.oth(0, 1)
    cot(0)
    act(2)
    gg.oth(1, 2)
    gg.own(1, 3)
    gg.own(0, 4)
    act(1)
    gg.oth(0, 2)
    act(3)
    branch(1)
    branch(0)
    out.hops(0, 4, 1)
    out.hops(0, 4, 0)
    out.hops(1, 4, 0)
    out.hops(1, 4, 1)
    gg.own(1, 4)
    cot(1)
    gg.oth(0, 3)
    gg.oth(1, 3)
    turn(2)
    act_back(0)
    turn(0)
    turn(3)
    gg.far(0, 4)
    cot(2)
    out.hops(0, 3, 1)
    out.hops(1, 3, 0)
    gg.far(1, 4)
    cot(3)
    out.hops(1, 3, 1)
    out.hops(0, 3, 0)
    act_back(1)
    out.hops(0, 2, 1)
    turn(1)
    w_out.give(hid_t, cots)
    out.hops(1, 2, 1)
    act_back(3)
    out.hops(0, 2, 0)
    out.hops(0, 1, 1)
    turn_back(0)
    turn_back(1)
    out.hops(1, 1, 1)
    out.hops(1, 2, 0)
    out.hops(0, 1, 0)
    turn_back(3)
    out.cross(0)
    act_back(2)
    back_prod(1)
    back_prod(0)
    back.hops(1, 4, 0)
    back.hops(0, 4, 1)
    turn_back(2)
    back.hops(1, 4, 1)
    w_in.give(dpre_t, acts)
    back.hops(0, 4, 0)
    back.hops(0, 3, 1)
    back.hops(1, 3, 1)
    back.hops(0, 3, 0)
    back.hops(0, 2, 1)
    back.hops(1, 2, 1)
    back.hops(1, 3, 0)
    back.hops(0, 1, 1)
    back.hops(1, 1, 1)
    back.hops(0, 2, 0)
    back.hops(1, 2, 0)
    back.cross(0)
    back.hops(0, 1, 0)
    out.cross(1)
    out.hops(1, 1, 0)
    back.cross(1)
    back.hops(1, 1, 0)
    out.rows(0)
    store_out_grad()
    store_in_grad()
    back.rows(0)
    out.rows(1)
    back.rows(1)

    for copy in pending:
        copy.wait_send()
    for copy in (store_out, store_in, *out.keep.values(), *back.keep.values()):
        copy.wait()


def local(block_in, norm_gain, weight_in, weight_out, output_grad):
    hbm = pl.BlockSpec(memory_space=pl.ANY)
    rows, width = block_in.shape
    half = 2 * UNITS
    gain = norm_gain.reshape(1, width)

    def buf(*shape, dtype=BF16):
        return pltpu.VMEM(shape, dtype)

    quarter = BLOCK // NX
    inputs = dict(x=buf(rows, width), gain=buf(1, width, dtype=F32), g=buf(rows, width))
    scratch = dict(
        **inputs, wi=buf(NX, WIDE, UNITS), wo=buf(NX, UNITS, WIDE),
        msg=buf(NX, 2 * ROWS, WIDE), got=buf(NX, 2 * ROWS, WIDE),
        acts=buf(2, 32, CHUNK, SIDE), cots=buf(2, 32, CHUNK, SIDE),
        terms=buf(2, 4, NX, quarter, UNITS), terms_in=buf(2, 4, NX - 1, quarter, UNITS),
        slope=buf(4, quarter, UNITS, dtype=F32),
        hid=buf(4, NX, quarter, UNITS), dpre=buf(4, NX, quarter, UNITS),
        hid_t=buf(UNITS, 4 * BLOCK), dpre_t=buf(UNITS, 4 * BLOCK),
        prod=buf(2, 2, 2, 2 * NZ, UNIT, WIDE), prod_sib=buf(2, 2, 2 * NZ, UNIT, WIDE),
        ring_in=buf(2, 2, 2, 4, 2, UNIT, WIDE), ring_out=buf(2, 2, 2, 4, 2, UNIT, WIDE),
        y_out=buf(2, 2, UNIT, WIDE), y_in=buf(2, 2, UNIT, WIDE),
        rows_out=buf(2, NX, ROWS, WIDE, dtype=F32),
        gsum=buf(2, 2, UNITS, half, dtype=F32), gsend=buf(2, UNITS, half),
        gin_got=buf(2, UNITS, half), gres=buf(2, UNITS, half, dtype=F32),
        ssem=pltpu.SemaphoreType.DMA((SEMS,)), rsem=pltpu.SemaphoreType.DMA((SEMS,)),
        lsem=pltpu.SemaphoreType.DMA((13,)), ksem=pltpu.SemaphoreType.DMA((2, 2)),
    )
    summed, gin_t, gout = pl.pallas_call(
        kernel,
        name="block",
        out_shape=(
            jax.ShapeDtypeStruct((2, NX, rows, WIDE), F32),
            jax.ShapeDtypeStruct((UNITS, half), F32),
            jax.ShapeDtypeStruct((UNITS, half), F32),
        ),
        in_specs=[hbm] * 5,
        out_specs=(hbm,) * 3,
        scratch_shapes=list(scratch.values()),
        compiler_params=pltpu.CompilerParams(
            collective_id=0, has_side_effects=True, vmem_limit_bytes=VMEM_ASKED
        ),
    )(block_in, gain, weight_in, weight_out, output_grad)
    return pl.pallas_call(
        finish_kernel,
        name="finish",
        out_shape=(
            jax.ShapeDtypeStruct((rows, width), BF16),
            jax.ShapeDtypeStruct((rows, width), BF16),
            jax.ShapeDtypeStruct((half, UNITS), F32),
            jax.ShapeDtypeStruct((UNITS, half), F32),
        ),
        in_specs=[hbm] * 6,
        out_specs=(hbm,) * 4,
        scratch_shapes=[
            *inputs.values(), buf(2, NX, rows, WIDE, dtype=F32), buf(UNITS, half, dtype=F32),
            buf(half, UNITS, dtype=F32), buf(UNITS, half, dtype=F32), buf(rows, width),
            buf(rows, width), pltpu.SemaphoreType.DMA((6,)), pltpu.SemaphoreType.DMA((4,)),
        ],
        compiler_params=pltpu.CompilerParams(vmem_limit_bytes=VMEM_ASKED),
    )(block_in, gain, output_grad, summed, gin_t, gout)


def solution(mesh):
    in_specs = (P(("dp", "mp"), None), P(), P(None, "mp"), P("mp", None), P(("dp", "mp"), None))
    out_specs = (P(("dp", "mp"), None), P(("dp", "mp"), None), P("dp", "mp"), P("mp", "dp"))
    return jax.shard_map(local, mesh=mesh, in_specs=in_specs, out_specs=out_specs, check_vma=False)
```

```python
import jax
import jax.numpy as jnp
from jax import lax
from jax.experimental import pallas as pl
from jax.experimental.pallas import tpu as pltpu
from jax.sharding import PartitionSpec as P

MESH = pl.DeviceIdType.MESH
F32, BF16 = jnp.float32, jnp.bfloat16

NX, NZ = 4, 8
ROWS = 8
CHUNK = NX * ROWS
WIDE = 1536
UNITS = 384
BLOCK = 256
SIDE = WIDE // 2
UNIT = 2 * ROWS
PER = BLOCK // (4 * CHUNK)
FAR = 4
SEMS = 320
VMEM_ASKED = 60 * 2**20


def place():
    dp, mp = lax.axis_index("dp"), lax.axis_index("mp")
    return (
        lax.div(dp, 2),
        lax.rem(dp, 2),
        lax.div(mp, 16),
        lax.rem(lax.div(mp, 2), NZ),
        lax.rem(mp, 2),
    )


def device(x, yl, yh, z, c):
    return (x * 2 + yl, (yh * NZ + z) * 2 + c)


def slot(way, dist):
    if dist == 0:
        return 0
    if dist == 4:
        return 7
    return 2 * dist - 1 + way


def dot(left, right, dims=((1,), (0,))):
    return lax.dot_general(left, right, (dims, ((), ())), preferred_element_type=F32)


def standardise(x_ref):
    values = x_ref[...].astype(F32)
    average = jnp.mean(values, axis=1, keepdims=True)
    centred = values - average
    inv_scale = lax.rsqrt(jnp.mean(centred * centred, axis=1, keepdims=True) + 1e-06)
    return centred * inv_scale, inv_scale


def finish_kernel(
    x_any, gain_any, g_any, rows_any, gin_any, gout_any,
    mixed_any, igrad_any, gin_out, gout_out,
    x_ref, gain_ref, g_ref, rows, gin, turned, gout, mixed, igrad, sems, osems,
):
    pairs = (
        (gin_any, gin), (x_any, x_ref), (gain_any, gain_ref), (g_any, g_ref), (rows_any, rows),
        (gout_any, gout))
    loads = [pltpu.make_async_copy(a, b, sems.at[k]) for k, (a, b) in enumerate(pairs)]
    for copy in loads:
        copy.start()
    stores = [
        pltpu.make_async_copy(a, b, osems.at[k])
        for k, (a, b) in enumerate((
            (turned, gin_out), (mixed, mixed_any), (igrad, igrad_any), (gout, gout_out)))]
    loads[0].wait()
    turned[...] = gin[...].T
    stores[0].start()
    for copy in loads[1:]:
        copy.wait()
    stores[3].start()
    width = x_ref.shape[1]
    for a in range(NX):
        cols = slice(a * WIDE, (a + 1) * WIDE)
        mixed[:, cols] = (x_ref[:, cols].astype(F32) + rows[0, a]).astype(BF16)
    stores[1].start()
    standard, inv_scale = standardise(x_ref)
    scaled = [rows[1, a] * gain_ref[:, a * WIDE:(a + 1) * WIDE] for a in range(NX)]
    standards = [standard[:, a * WIDE:(a + 1) * WIDE] for a in range(NX)]
    mean_scaled = sum(jnp.sum(s, axis=1, keepdims=True) for s in scaled) / width
    mean_both = sum(
        jnp.sum(s * t, axis=1, keepdims=True) for s, t in zip(scaled, standards)) / width
    for a in range(NX):
        cols = slice(a * WIDE, (a + 1) * WIDE)
        change = inv_scale * (scaled[a] - mean_scaled - standards[a] * mean_both)
        igrad[:, cols] = (g_ref[:, cols].astype(F32) + change).astype(BF16)
    stores[2].start()
    for copy in stores:
        copy.wait()


def kernel(
    x_any, gain_any, wi_any, wo_any, g_any,
    rows_any, gin_any, gout_any,
    x_ref, gain_ref, g_ref, wi, wo, msg, got, acts, cots,
    terms, terms_in, slope, hid, dpre, hid_t, dpre_t,
    prod, prod_sib, ring_in, ring_out, y_out, y_in, rows_out,
    gsum, gsend, gin_got, gres,
    ssem, rsem, lsem, ksem,
):
    x, yl, yh, z, c = place()
    xs = [lax.rem(x + k, NX) for k in range(NX)]
    zp, zm = lax.rem(z + 1, NZ), lax.rem(z + NZ - 1, NZ)
    to_z = (device(x, yl, yh, zp, c), device(x, yl, yh, zm, c))
    to_sib = device(x, yl, yh, z, 1 - c)
    to_yh = device(x, yl, 1 - yh, z, c)
    to_yl = device(x, 1 - yl, yh, z, c)
    to_x = [device(xs[k], yl, yh, z, c) for k in range(NX)]

    barrier = pltpu.get_barrier_semaphore()
    for other in (*to_z, to_sib, to_yh, to_yl, *to_x[1:]):
        pl.semaphore_signal(barrier, inc=1, device_id=other, device_id_type=MESH)

    weights = []
    for a in range(NX):
        cols = pl.ds(a * WIDE, WIDE)
        weights.append(pltpu.make_async_copy(wi_any.at[cols], wi.at[a], lsem.at[5 + a]))
        weights.append(pltpu.make_async_copy(wo_any.at[:, cols], wo.at[a], lsem.at[9 + a]))

    loads = [
        pltpu.make_async_copy(src, dst, lsem.at[2 + k])
        for k, (src, dst) in enumerate(((x_any, x_ref), (gain_any, gain_ref), (g_any, g_ref)))]
    for copy in loads:
        copy.start()
    for copy in weights:
        copy.start()
    for copy in loads:
        copy.wait()

    normed = standardise(x_ref)[0] * gain_ref[...]
    grad = g_ref[...].astype(F32)
    for q in range(NX):
        cols = slice(q * WIDE, (q + 1) * WIDE)
        msg[q] = jnp.concatenate([normed[:, cols], grad[:, cols]], axis=0).astype(BF16)

    pl.semaphore_wait(barrier, 8)

    pending = []

    def send(src, dst, to):
        k = len(pending)
        copy = pltpu.make_async_remote_copy(
            src_ref=src, dst_ref=dst, send_sem=ssem.at[k], recv_sem=rsem.at[k],
            device_id=to, device_id_type=MESH)
        copy.start()
        pending.append(copy)
        return copy

    first = [send(msg.at[xs[k]], got.at[x], to_x[k]) for k in range(1, NX)]
    got[x] = msg[x]
    for copy in first:
        copy.wait_recv()
    pieces = [got[a].astype(F32) for a in range(NX)]
    for part in (0, 1):
        cols = slice(part * SIDE, (part + 1) * SIDE)
        acts[part, 0] = jnp.concatenate([p[:ROWS, cols] for p in pieces], axis=0).astype(BF16)
        cots[part, 0] = jnp.concatenate([p[ROWS:, cols] for p in pieces], axis=0).astype(BF16)

    def ways(dist, part, turn):
        return (0, 1) if dist < 4 else (part ^ turn,)

    class Gather:
        def __init__(self, buf, turn):
            self.buf, self.turn = buf, turn
            self.near, self.ring, self.y, self.sib = {}, {}, {}, {}

        def at(self, part, s, h):
            return self.buf.at[part, 4 * s + h]

        def pass_on(self, part, way, dist, h):
            here = self.at(part, slot(way, dist), h)
            if dist < (FAR - 1 if h else 4) and way in ways(dist + 1, part, self.turn):
                there = self.at(part, slot(way, dist + 1), h)
                self.ring[part, way, dist + 1, h] = send(here, there, to_z[way])
            if dist >= FAR and h == 0:
                there = self.at(part, slot(way, dist), 1)
                self.y[part, way, dist] = send(here, there, to_yh)

        def to_core(self, part, s):
            self.sib[part, s] = send(
                self.buf.at[part, pl.ds(4 * s, 2)], self.buf.at[part, pl.ds(4 * s + 2, 2)], to_sib)

        def start(self, part):
            self.near[part] = send(self.at(part, 0, 0), self.at(part, 0, 1), to_yh)
            for way in (0, 1):
                self.pass_on(part, way, 0, 0)

        def other(self, part):
            self.near[part].wait_recv()
            for way in (0, 1):
                self.pass_on(part, way, 0, 1)
            self.to_core(part, 0)

        def own(self, part, dist):
            for way in ways(dist, part, self.turn):
                self.ring[part, way, dist, 0].wait_recv()
                self.pass_on(part, way, dist, 0)

        def oth(self, part, dist):
            for way in (0, 1):
                self.ring[part, way, dist, 1].wait_recv()
                self.pass_on(part, way, dist, 1)
                self.to_core(part, slot(way, dist))

        def far(self, part, dist):
            for way in ways(dist, part, self.turn):
                self.y[part, way, dist].wait_recv()
                self.to_core(part, slot(way, dist))

        def block(self, b):
            for s in range(PER * b, PER * b + PER):
                for part in (0, 1):
                    self.sib[part, s].wait_recv()
            return [
                self.buf[part, 8 * b:8 * b + 8].reshape(BLOCK, SIDE) for part in (0, 1)]

    class Across:
        def __init__(self, i, result):
            self.term, self.came, self.result = terms.at[i], terms_in.at[i], result
            self.out, self.back = {}, {}

        def give(self, b, term):
            term = term.reshape(8, NX, ROWS, UNITS)
            for q in range(NX):
                self.term[b, q] = term[:, q].reshape(8 * ROWS, UNITS).astype(BF16)
            self.out[b] = [
                send(self.term.at[b, xs[k]], self.came.at[b, k - 1], to_x[k]) for k in range(1, NX)]

        def total(self, b):
            for copy in self.out[b]:
                copy.wait_recv()
            total = self.term[b, x].astype(F32)
            for k in range(NX - 1):
                total = total + self.came[b, k].astype(F32)
            return total

        def keep(self, b, value):
            self.result[b, x] = value.astype(BF16)

        def share(self, b):
            self.back[b] = [
                send(self.result.at[b, x], self.result.at[b, x], to_x[k]) for k in range(1, NX)]

        def own(self):
            return self.result[:, x].reshape(BLOCK, UNITS)

        def turned(self, b):
            for copy in self.back[b]:
                copy.wait_recv()
            value = self.result[b].astype(F32).reshape(NX, 8, ROWS, UNITS)
            rows = [value[q, k] for k in range(8) for q in range(NX)]
            return jnp.concatenate(rows, axis=0).T.astype(BF16)

    class Scatter:
        def __init__(self, i, turn):
            self.turn = turn
            self.prod, self.sib = prod.at[i], prod_sib.at[i]
            self.rin, self.rout = ring_in.at[i], ring_out.at[i]
            self.yout, self.yin = y_out.at[i], y_in.at[i]
            self.rows_out, self.rows_hbm = rows_out.at[i], rows_any.at[i]
            self.sibs, self.ring, self.y, self.seen = {}, {}, {}, set()
            self.keep, self.keep_sem = {}, ksem.at[i]

        def give(self, part, left, right, turned):
            for n in range(0, WIDE, 512):
                pair = []
                for a in (2 * part, 2 * part + 1):
                    if turned:
                        term = dot(left, right[a, n:n + 512, :], ((1,), (1,)))
                    else:
                        term = dot(left, right[a, :, n:n + 512])
                    pair.append(term.reshape(NZ, 2, 2, ROWS, 512))
                term = jnp.concatenate(pair, axis=3).astype(BF16)
                for core in (0, 1):
                    rows = term[:, core].reshape(2 * NZ, UNIT, 512)
                    self.prod[core, part, :, :, n:n + 512] = rows
            for k in (1, 0):
                rows = pl.ds(NZ * k, NZ)
                self.sibs[part, k] = send(
                    self.prod.at[1, part, rows], self.sib.at[part, rows], to_sib)

        def term(self, part, s, h):
            k, q = s // 4, 2 * s + h
            if (part, k) not in self.seen:
                self.seen.add((part, k))
                self.sibs[part, k].wait_recv()
            return self.prod[0, part, q].astype(F32) + self.sib[part, q].astype(F32)

        def hop(self, part, way, dist, h):
            value = self.term(part, slot(way, dist), h)
            if (part, way, dist, h) in self.ring:
                self.ring[part, way, dist, h].wait_recv()
                value = value + self.rin[part, way, dist, h].astype(F32)
            self.rout[part, way, dist - 1, h] = value.astype(BF16)
            self.ring[part, way, dist - 1, h] = send(
                self.rout.at[part, way, dist - 1, h], self.rin.at[part, way, dist - 1, h],
                to_z[1 - way])

        def hops(self, part, dist, h):
            for way in ways(dist, part, self.turn):
                self.hop(part, way, dist, h)

        def near(self, part, h):
            value = self.term(part, 0, h)
            for way in (0, 1):
                self.ring[part, way, 0, h].wait_recv()
                value = value + self.rin[part, way, 0, h].astype(F32)
            return value

        def cross(self, part):
            self.yout[part] = self.near(part, 1).astype(BF16)
            self.y[part] = send(self.yout.at[part], self.yin.at[part], to_yh)

        def rows(self, part):
            value = self.near(part, 0)
            self.y[part].wait_recv()
            value = value + self.yin[part].astype(F32)
            self.rows_out[2 * part:2 * part + 2] = value.reshape(2, ROWS, WIDE)
            cols = pl.ds(2 * part, 2)
            self.keep[part] = pltpu.make_async_copy(
                self.rows_out.at[cols], self.rows_hbm.at[cols], self.keep_sem.at[part])
            self.keep[part].start()

    class Weights:
        def __init__(self, i):
            self.sum, self.out, self.came = gsum.at[i], gsend.at[i], gin_got.at[i]

        def give(self, left_t, right):
            left = left_t[...]
            for n in range(4):
                cols = slice((n % 2) * UNITS, (n % 2 + 1) * UNITS)
                term = dot(left, right[n // 2, :, :, cols].reshape(4 * BLOCK, UNITS))
                self.sum[n // 2, :, cols] = term
            self.out[...] = self.sum[1 - yl].astype(BF16)
            self.copy = send(self.out, self.came, to_yl)

        def total(self):
            self.copy.wait_recv()
            return self.sum[yl] + self.came[...].astype(F32)

    ga, gg = Gather(acts, 0), Gather(cots, 1)
    fwd, bwd = Across(0, hid), Across(1, dpre)
    out, back = Scatter(0, 0), Scatter(1, 1)
    w_out, w_in = Weights(0), Weights(1)

    def pre(b):
        sides = ga.block(b)
        fwd.give(b, dot(sides[0], wi[x, :SIDE]) + dot(sides[1], wi[x, SIDE:]))

    def act(b):
        value = fwd.total(b)
        cdf = 0.5 * (1.0 + lax.erf(value * 0.7071067811865476))
        slope[b] = cdf + value * jnp.exp(-0.5 * value * value) * 0.3989422804014327
        fwd.keep(b, value * cdf)

    def cot(b):
        sides, dims = gg.block(b), ((1,), (1,))
        bwd.give(b, dot(sides[0], wo[x, :, :SIDE], dims) + dot(sides[1], wo[x, :, SIDE:], dims))

    def act_back(b):
        bwd.keep(b, bwd.total(b) * slope[b])

    def branch(part):
        out.give(part, fwd.own(), wo, False)

    def back_prod(part):
        back.give(part, bwd.own(), wi, True)

    def turn(b):
        hid_t[:, b * BLOCK:(b + 1) * BLOCK] = fwd.turned(b)

    def turn_back(b):
        dpre_t[:, b * BLOCK:(b + 1) * BLOCK] = bwd.turned(b)

    def store_out_grad():
        gres[0] = w_out.total()
        store_out.start()

    def store_in_grad():
        gres[1] = w_in.total()
        store_in.start()

    store_out = pltpu.make_async_copy(gres.at[0], gout_any, lsem.at[0])
    store_in = pltpu.make_async_copy(gres.at[1], gin_any, lsem.at[1])

    ga.start(1)
    ga.start(0)
    gg.start(0)
    ga.own(1, 1)
    ga.own(0, 1)
    ga.other(1)
    ga.other(0)
    ga.own(1, 2)
    ga.own(0, 2)
    ga.oth(1, 1)
    ga.oth(0, 1)
    ga.own(1, 3)
    gg.start(1)
    for copy in weights:
        copy.wait()
    pre(0)
    ga.own(0, 3)
    ga.oth(1, 2)
    ga.oth(0, 2)
    gg.own(0, 1)
    ga.own(1, 4)
    gg.other(1)
    pre(1)
    ga.own(0, 4)
    act(0)
    ga.oth(1, 3)
    gg.own(1, 1)
    fwd.share(0)
    ga.oth(0, 3)
    gg.other(0)
    gg.own(0, 2)
    ga.far(1, 4)
    pre(2)
    ga.far(0, 4)
    act(1)
    gg.own(1, 2)
    gg.oth(1, 1)
    pre(3)
    fwd.share(1)
    gg.own(0, 3)
    gg.oth(0, 1)
    gg.own(1, 3)
    act(2)
    turn(0)
    fwd.share(2)
    gg.oth(1, 2)
    gg.own(0, 4)
    act(3)
    fwd.share(3)
    branch(0)
    gg.own(1, 4)
    gg.oth(0, 2)
    branch(1)
    cot(0)
    out.hops(0, 4, 1)
    gg.oth(1, 3)
    gg.far(0, 4)
    turn(2)
    cot(1)
    gg.oth(0, 3)
    turn(3)
    gg.far(1, 4)
    turn(1)
    out.hops(1, 4, 1)
    cot(2)
    out.hops(0, 3, 1)
    cot(3)
    w_out.give(hid_t, cots)
    out.hops(1, 4, 0)
    out.hops(0, 4, 0)
    act_back(0)
    act_back(1)
    bwd.share(0)
    out.hops(1, 3, 1)
    act_back(2)
    out.hops(0, 2, 1)
    bwd.share(2)
    act_back(3)
    bwd.share(3)
    out.hops(0, 3, 0)
    out.hops(1, 3, 0)
    back_prod(0)
    bwd.share(1)
    out.hops(0, 1, 1)
    back_prod(1)
    out.hops(1, 2, 1)
    turn_back(0)
    back.hops(0, 4, 1)
    back.hops(0, 4, 0)
    out.hops(0, 2, 0)
    turn_back(2)
    out.cross(0)
    back.hops(1, 4, 0)
    back.hops(1, 4, 1)
    out.hops(1, 2, 0)
    turn_back(3)
    turn_back(1)
    w_in.give(dpre_t, acts)
    back.hops(0, 3, 1)
    back.hops(1, 3, 1)
    back.hops(0, 3, 0)
    out.hops(0, 1, 0)
    back.hops(0, 2, 1)
    out.hops(1, 1, 1)
    back.hops(1, 2, 1)
    back.hops(1, 3, 0)
    back.hops(0, 2, 0)
    store_out_grad()
    back.hops(0, 1, 1)
    out.cross(1)
    back.hops(1, 1, 1)
    back.hops(1, 2, 0)
    out.hops(1, 1, 0)
    back.hops(0, 1, 0)
    back.cross(0)
    out.rows(0)
    back.cross(1)
    back.hops(1, 1, 0)
    out.rows(1)
    store_in_grad()
    back.rows(0)
    back.rows(1)

    for copy in pending:
        copy.wait_send()
    for copy in (store_out, store_in, *out.keep.values(), *back.keep.values()):
        copy.wait()


def local(block_in, norm_gain, weight_in, weight_out, output_grad):
    hbm = pl.BlockSpec(memory_space=pl.ANY)
    rows, width = block_in.shape
    half = 2 * UNITS
    gain = norm_gain.reshape(1, width)

    def buf(*shape, dtype=BF16):
        return pltpu.VMEM(shape, dtype)

    quarter = BLOCK // NX
    inputs = dict(x=buf(rows, width), gain=buf(1, width, dtype=F32), g=buf(rows, width))
    scratch = dict(
        **inputs, wi=buf(NX, WIDE, UNITS), wo=buf(NX, UNITS, WIDE),
        msg=buf(NX, 2 * ROWS, WIDE), got=buf(NX, 2 * ROWS, WIDE),
        acts=buf(2, 32, CHUNK, SIDE), cots=buf(2, 32, CHUNK, SIDE),
        terms=buf(2, 4, NX, quarter, UNITS), terms_in=buf(2, 4, NX - 1, quarter, UNITS),
        slope=buf(4, quarter, UNITS, dtype=F32),
        hid=buf(4, NX, quarter, UNITS), dpre=buf(4, NX, quarter, UNITS),
        hid_t=buf(UNITS, 4 * BLOCK), dpre_t=buf(UNITS, 4 * BLOCK),
        prod=buf(2, 2, 2, 2 * NZ, UNIT, WIDE), prod_sib=buf(2, 2, 2 * NZ, UNIT, WIDE),
        ring_in=buf(2, 2, 2, 4, 2, UNIT, WIDE), ring_out=buf(2, 2, 2, 4, 2, UNIT, WIDE),
        y_out=buf(2, 2, UNIT, WIDE), y_in=buf(2, 2, UNIT, WIDE),
        rows_out=buf(2, NX, ROWS, WIDE, dtype=F32),
        gsum=buf(2, 2, UNITS, half, dtype=F32), gsend=buf(2, UNITS, half),
        gin_got=buf(2, UNITS, half), gres=buf(2, UNITS, half, dtype=F32),
        ssem=pltpu.SemaphoreType.DMA((SEMS,)), rsem=pltpu.SemaphoreType.DMA((SEMS,)),
        lsem=pltpu.SemaphoreType.DMA((13,)), ksem=pltpu.SemaphoreType.DMA((2, 2)),
    )
    summed, gin_t, gout = pl.pallas_call(
        kernel,
        name="block",
        out_shape=(
            jax.ShapeDtypeStruct((2, NX, rows, WIDE), F32),
            jax.ShapeDtypeStruct((UNITS, half), F32),
            jax.ShapeDtypeStruct((UNITS, half), F32),
        ),
        in_specs=[hbm] * 5,
        out_specs=(hbm,) * 3,
        scratch_shapes=list(scratch.values()),
        compiler_params=pltpu.CompilerParams(
            collective_id=0, has_side_effects=True, vmem_limit_bytes=VMEM_ASKED
        ),
    )(block_in, gain, weight_in, weight_out, output_grad)
    return pl.pallas_call(
        finish_kernel,
        name="finish",
        out_shape=(
            jax.ShapeDtypeStruct((rows, width), BF16),
            jax.ShapeDtypeStruct((rows, width), BF16),
            jax.ShapeDtypeStruct((half, UNITS), F32),
            jax.ShapeDtypeStruct((UNITS, half), F32),
        ),
        in_specs=[hbm] * 6,
        out_specs=(hbm,) * 4,
        scratch_shapes=[
            *inputs.values(), buf(2, NX, rows, WIDE, dtype=F32), buf(UNITS, half, dtype=F32),
            buf(half, UNITS, dtype=F32), buf(UNITS, half, dtype=F32), buf(rows, width),
            buf(rows, width), pltpu.SemaphoreType.DMA((6,)), pltpu.SemaphoreType.DMA((4,)),
        ],
        compiler_params=pltpu.CompilerParams(vmem_limit_bytes=VMEM_ASKED),
    )(block_in, gain, output_grad, summed, gin_t, gout)


def solution(mesh):
    in_specs = (P(("dp", "mp"), None), P(), P(None, "mp"), P("mp", None), P(("dp", "mp"), None))
    out_specs = (P(("dp", "mp"), None), P(("dp", "mp"), None), P("dp", "mp"), P("mp", "dp"))
    return jax.shard_map(local, mesh=mesh, in_specs=in_specs, out_specs=out_specs, check_vma=False)
```

```python
import jax
import jax.numpy as jnp
from jax import lax
from jax.experimental import pallas as pl
from jax.experimental.pallas import tpu as pltpu
from jax.sharding import PartitionSpec as P

MESH = pl.DeviceIdType.MESH
F32, BF16 = jnp.float32, jnp.bfloat16

NX, NZ = 4, 8
ROWS = 8
CHUNK = NX * ROWS
WIDE = 1536
UNITS = 384
BLOCK = 256
SIDE = WIDE // 2
UNIT = 2 * ROWS
PER = BLOCK // (4 * CHUNK)
FAR = 3
SEMS = 320
VMEM_ASKED = 60 * 2**20


def place():
    dp, mp = lax.axis_index("dp"), lax.axis_index("mp")
    return (
        lax.div(dp, 2),
        lax.rem(dp, 2),
        lax.div(mp, 16),
        lax.rem(lax.div(mp, 2), NZ),
        lax.rem(mp, 2),
    )


def device(x, yl, yh, z, c):
    return (x * 2 + yl, (yh * NZ + z) * 2 + c)


def slot(way, dist):
    if dist == 0:
        return 0
    if dist == 4:
        return 7
    return 2 * dist - 1 + way


def dot(left, right, dims=((1,), (0,))):
    return lax.dot_general(left, right, (dims, ((), ())), preferred_element_type=F32)


def standardise(x_ref):
    values = x_ref[...].astype(F32)
    average = jnp.mean(values, axis=1, keepdims=True)
    centred = values - average
    inv_scale = lax.rsqrt(jnp.mean(centred * centred, axis=1, keepdims=True) + 1e-06)
    return centred * inv_scale, inv_scale


def finish_kernel(
    x_any, gain_any, g_any, rows_any, gin_any, gout_any,
    mixed_any, igrad_any, gin_out, gout_out,
    x_ref, gain_ref, g_ref, rows, gin, turned, gout, mixed, igrad, sems, osems,
):
    pairs = (
        (gin_any, gin), (x_any, x_ref), (gain_any, gain_ref), (g_any, g_ref), (rows_any, rows),
        (gout_any, gout))
    loads = [pltpu.make_async_copy(a, b, sems.at[k]) for k, (a, b) in enumerate(pairs)]
    for copy in loads:
        copy.start()
    stores = [
        pltpu.make_async_copy(a, b, osems.at[k])
        for k, (a, b) in enumerate((
            (turned, gin_out), (mixed, mixed_any), (igrad, igrad_any), (gout, gout_out)))]
    loads[0].wait()
    turned[...] = gin[...].T
    stores[0].start()
    for copy in loads[1:]:
        copy.wait()
    stores[3].start()
    width = x_ref.shape[1]
    for a in range(NX):
        cols = slice(a * WIDE, (a + 1) * WIDE)
        mixed[:, cols] = (x_ref[:, cols].astype(F32) + rows[0, a]).astype(BF16)
    stores[1].start()
    standard, inv_scale = standardise(x_ref)
    scaled = [rows[1, a] * gain_ref[:, a * WIDE:(a + 1) * WIDE] for a in range(NX)]
    standards = [standard[:, a * WIDE:(a + 1) * WIDE] for a in range(NX)]
    mean_scaled = sum(jnp.sum(s, axis=1, keepdims=True) for s in scaled) / width
    mean_both = sum(
        jnp.sum(s * t, axis=1, keepdims=True) for s, t in zip(scaled, standards)) / width
    for a in range(NX):
        cols = slice(a * WIDE, (a + 1) * WIDE)
        change = inv_scale * (scaled[a] - mean_scaled - standards[a] * mean_both)
        igrad[:, cols] = (g_ref[:, cols].astype(F32) + change).astype(BF16)
    stores[2].start()
    for copy in stores:
        copy.wait()


def kernel(
    x_any, gain_any, wi_any, wo_any, g_any,
    rows_any, gin_any, gout_any,
    x_ref, gain_ref, g_ref, wi, wo, msg, got, acts, cots,
    terms, terms_in, slope, hid, dpre, hid_t, dpre_t,
    prod, prod_sib, ring_in, ring_out, y_out, y_in, rows_out,
    gsum, gsend, gin_got, gres,
    ssem, rsem, lsem, ksem,
):
    x, yl, yh, z, c = place()
    xs = [lax.rem(x + k, NX) for k in range(NX)]
    zp, zm = lax.rem(z + 1, NZ), lax.rem(z + NZ - 1, NZ)
    to_z = (device(x, yl, yh, zp, c), device(x, yl, yh, zm, c))
    to_sib = device(x, yl, yh, z, 1 - c)
    to_yh = device(x, yl, 1 - yh, z, c)
    to_yl = device(x, 1 - yl, yh, z, c)
    to_x = [device(xs[k], yl, yh, z, c) for k in range(NX)]

    barrier = pltpu.get_barrier_semaphore()
    for other in (*to_z, to_sib, to_yh, to_yl, *to_x[1:]):
        pl.semaphore_signal(barrier, inc=1, device_id=other, device_id_type=MESH)

    weights = []
    for a in range(NX):
        cols = pl.ds(a * WIDE, WIDE)
        weights.append(pltpu.make_async_copy(wi_any.at[cols], wi.at[a], lsem.at[5 + a]))
        weights.append(pltpu.make_async_copy(wo_any.at[:, cols], wo.at[a], lsem.at[9 + a]))

    loads = [
        pltpu.make_async_copy(src, dst, lsem.at[2 + k])
        for k, (src, dst) in enumerate(((x_any, x_ref), (gain_any, gain_ref), (g_any, g_ref)))]
    for copy in loads:
        copy.start()
    for copy in weights:
        copy.start()
    for copy in loads:
        copy.wait()

    normed = standardise(x_ref)[0] * gain_ref[...]
    grad = g_ref[...].astype(F32)
    for q in range(NX):
        cols = slice(q * WIDE, (q + 1) * WIDE)
        msg[q] = jnp.concatenate([normed[:, cols], grad[:, cols]], axis=0).astype(BF16)

    pl.semaphore_wait(barrier, 8)

    pending = []

    def send(src, dst, to):
        k = len(pending)
        copy = pltpu.make_async_remote_copy(
            src_ref=src, dst_ref=dst, send_sem=ssem.at[k], recv_sem=rsem.at[k],
            device_id=to, device_id_type=MESH)
        copy.start()
        pending.append(copy)
        return copy

    first = [send(msg.at[xs[k]], got.at[x], to_x[k]) for k in range(1, NX)]
    got[x] = msg[x]
    for copy in first:
        copy.wait_recv()
    pieces = [got[a].astype(F32) for a in range(NX)]
    for part in (0, 1):
        cols = slice(part * SIDE, (part + 1) * SIDE)
        acts[part, 0] = jnp.concatenate([p[:ROWS, cols] for p in pieces], axis=0).astype(BF16)
        cots[part, 0] = jnp.concatenate([p[ROWS:, cols] for p in pieces], axis=0).astype(BF16)

    def ways(dist, part, turn):
        return (0, 1) if dist < 4 else (part ^ turn,)

    class Gather:
        def __init__(self, buf, turn):
            self.buf, self.turn = buf, turn
            self.near, self.ring, self.y, self.sib = {}, {}, {}, {}

        def at(self, part, s, h):
            return self.buf.at[part, 4 * s + h]

        def pass_on(self, part, way, dist, h):
            here = self.at(part, slot(way, dist), h)
            if dist < (FAR - 1 if h else 4) and way in ways(dist + 1, part, self.turn):
                there = self.at(part, slot(way, dist + 1), h)
                self.ring[part, way, dist + 1, h] = send(here, there, to_z[way])
            if dist >= FAR and h == 0:
                there = self.at(part, slot(way, dist), 1)
                self.y[part, way, dist] = send(here, there, to_yh)

        def to_core(self, part, s):
            self.sib[part, s] = send(
                self.buf.at[part, pl.ds(4 * s, 2)], self.buf.at[part, pl.ds(4 * s + 2, 2)], to_sib)

        def start(self, part):
            self.near[part] = send(self.at(part, 0, 0), self.at(part, 0, 1), to_yh)
            for way in (0, 1):
                self.pass_on(part, way, 0, 0)

        def other(self, part):
            self.near[part].wait_recv()
            for way in (0, 1):
                self.pass_on(part, way, 0, 1)
            self.to_core(part, 0)

        def own(self, part, dist):
            for way in ways(dist, part, self.turn):
                self.ring[part, way, dist, 0].wait_recv()
                self.pass_on(part, way, dist, 0)

        def oth(self, part, dist):
            for way in (0, 1):
                self.ring[part, way, dist, 1].wait_recv()
                self.pass_on(part, way, dist, 1)
                self.to_core(part, slot(way, dist))

        def far(self, part, dist):
            for way in ways(dist, part, self.turn):
                self.y[part, way, dist].wait_recv()
                self.to_core(part, slot(way, dist))

        def block(self, b):
            for s in range(PER * b, PER * b + PER):
                for part in (0, 1):
                    self.sib[part, s].wait_recv()
            return [
                self.buf[part, 8 * b:8 * b + 8].reshape(BLOCK, SIDE) for part in (0, 1)]

    class Across:
        def __init__(self, i, result):
            self.term, self.came, self.result = terms.at[i], terms_in.at[i], result
            self.out, self.back = {}, {}

        def give(self, b, term):
            term = term.reshape(8, NX, ROWS, UNITS)
            for q in range(NX):
                self.term[b, q] = term[:, q].reshape(8 * ROWS, UNITS).astype(BF16)
            self.out[b] = [
                send(self.term.at[b, xs[k]], self.came.at[b, k - 1], to_x[k]) for k in range(1, NX)]

        def total(self, b):
            for copy in self.out[b]:
                copy.wait_recv()
            total = self.term[b, x].astype(F32)
            for k in range(NX - 1):
                total = total + self.came[b, k].astype(F32)
            return total

        def keep(self, b, value):
            self.result[b, x] = value.astype(BF16)

        def share(self, b):
            self.back[b] = [
                send(self.result.at[b, x], self.result.at[b, x], to_x[k]) for k in range(1, NX)]

        def own(self):
            return self.result[:, x].reshape(BLOCK, UNITS)

        def turned(self, b):
            for copy in self.back[b]:
                copy.wait_recv()
            value = self.result[b].astype(F32).reshape(NX, 8, ROWS, UNITS)
            rows = [value[q, k] for k in range(8) for q in range(NX)]
            return jnp.concatenate(rows, axis=0).T.astype(BF16)

    class Scatter:
        def __init__(self, i, turn):
            self.turn = turn
            self.prod, self.sib = prod.at[i], prod_sib.at[i]
            self.rin, self.rout = ring_in.at[i], ring_out.at[i]
            self.yout, self.yin = y_out.at[i], y_in.at[i]
            self.rows_out, self.rows_hbm = rows_out.at[i], rows_any.at[i]
            self.sibs, self.ring, self.y, self.seen = {}, {}, {}, set()
            self.keep, self.keep_sem = {}, ksem.at[i]

        def give(self, part, left, right, turned):
            for n in range(0, WIDE, 512):
                pair = []
                for a in (2 * part, 2 * part + 1):
                    if turned:
                        term = dot(left, right[a, n:n + 512, :], ((1,), (1,)))
                    else:
                        term = dot(left, right[a, :, n:n + 512])
                    pair.append(term.reshape(NZ, 2, 2, ROWS, 512))
                term = jnp.concatenate(pair, axis=3).astype(BF16)
                for core in (0, 1):
                    rows = term[:, core].reshape(2 * NZ, UNIT, 512)
                    self.prod[core, part, :, :, n:n + 512] = rows
            for k in (1, 0):
                rows = pl.ds(NZ * k, NZ)
                self.sibs[part, k] = send(
                    self.prod.at[1, part, rows], self.sib.at[part, rows], to_sib)

        def term(self, part, s, h):
            k, q = s // 4, 2 * s + h
            if (part, k) not in self.seen:
                self.seen.add((part, k))
                self.sibs[part, k].wait_recv()
            return self.prod[0, part, q].astype(F32) + self.sib[part, q].astype(F32)

        def hop(self, part, way, dist, h):
            value = self.term(part, slot(way, dist), h)
            if (part, way, dist, h) in self.ring:
                self.ring[part, way, dist, h].wait_recv()
                value = value + self.rin[part, way, dist, h].astype(F32)
            self.rout[part, way, dist - 1, h] = value.astype(BF16)
            self.ring[part, way, dist - 1, h] = send(
                self.rout.at[part, way, dist - 1, h], self.rin.at[part, way, dist - 1, h],
                to_z[1 - way])

        def hops(self, part, dist, h):
            for way in ways(dist, part, self.turn):
                self.hop(part, way, dist, h)

        def near(self, part, h):
            value = self.term(part, 0, h)
            for way in (0, 1):
                self.ring[part, way, 0, h].wait_recv()
                value = value + self.rin[part, way, 0, h].astype(F32)
            return value

        def cross(self, part):
            self.yout[part] = self.near(part, 1).astype(BF16)
            self.y[part] = send(self.yout.at[part], self.yin.at[part], to_yh)

        def rows(self, part):
            value = self.near(part, 0)
            self.y[part].wait_recv()
            value = value + self.yin[part].astype(F32)
            self.rows_out[2 * part:2 * part + 2] = value.reshape(2, ROWS, WIDE)
            cols = pl.ds(2 * part, 2)
            self.keep[part] = pltpu.make_async_copy(
                self.rows_out.at[cols], self.rows_hbm.at[cols], self.keep_sem.at[part])
            self.keep[part].start()

    class Weights:
        def __init__(self, i):
            self.sum, self.out, self.came = gsum.at[i], gsend.at[i], gin_got.at[i]

        def give(self, left_t, right):
            left = left_t[...]
            for n in range(4):
                cols = slice((n % 2) * UNITS, (n % 2 + 1) * UNITS)
                term = dot(left, right[n // 2, :, :, cols].reshape(4 * BLOCK, UNITS))
                self.sum[n // 2, :, cols] = term
            self.out[...] = self.sum[1 - yl].astype(BF16)
            self.copy = send(self.out, self.came, to_yl)

        def total(self):
            self.copy.wait_recv()
            return self.sum[yl] + self.came[...].astype(F32)

    ga, gg = Gather(acts, 0), Gather(cots, 1)
    fwd, bwd = Across(0, hid), Across(1, dpre)
    out, back = Scatter(0, 0), Scatter(1, 1)
    w_out, w_in = Weights(0), Weights(1)

    def pre(b):
        sides = ga.block(b)
        fwd.give(b, dot(sides[0], wi[x, :SIDE]) + dot(sides[1], wi[x, SIDE:]))

    def act(b):
        value = fwd.total(b)
        cdf = 0.5 * (1.0 + lax.erf(value * 0.7071067811865476))
        slope[b] = cdf + value * jnp.exp(-0.5 * value * value) * 0.3989422804014327
        fwd.keep(b, value * cdf)

    def cot(b):
        sides, dims = gg.block(b), ((1,), (1,))
        bwd.give(b, dot(sides[0], wo[x, :, :SIDE], dims) + dot(sides[1], wo[x, :, SIDE:], dims))

    def act_back(b):
        bwd.keep(b, bwd.total(b) * slope[b])

    def branch(part):
        out.give(part, fwd.own(), wo, False)

    def back_prod(part):
        back.give(part, bwd.own(), wi, True)

    def turn(b):
        hid_t[:, b * BLOCK:(b + 1) * BLOCK] = fwd.turned(b)

    def turn_back(b):
        dpre_t[:, b * BLOCK:(b + 1) * BLOCK] = bwd.turned(b)

    def store_out_grad():
        gres[0] = w_out.total()
        store_out.start()

    def store_in_grad():
        gres[1] = w_in.total()
        store_in.start()

    store_out = pltpu.make_async_copy(gres.at[0], gout_any, lsem.at[0])
    store_in = pltpu.make_async_copy(gres.at[1], gin_any, lsem.at[1])

    ga.start(1)
    ga.start(0)
    gg.start(1)
    ga.own(1, 1)
    ga.own(0, 1)
    ga.other(1)
    ga.own(1, 2)
    ga.own(0, 2)
    ga.other(0)
    gg.start(0)
    ga.own(1, 3)
    ga.own(0, 3)
    ga.oth(1, 1)
    ga.oth(0, 1)
    gg.own(1, 1)
    ga.own(1, 4)
    ga.own(0, 4)
    gg.own(0, 1)
    ga.oth(1, 2)
    for copy in weights:
        copy.wait()
    pre(0)
    ga.oth(0, 2)
    gg.other(1)
    ga.far(1, 3)
    gg.own(1, 2)
    ga.far(0, 3)
    pre(1)
    gg.own(0, 2)
    ga.far(1, 4)
    pre(2)
    ga.far(0, 4)
    gg.other(0)
    act(0)
    gg.own(1, 3)
    gg.oth(1, 1)
    pre(3)
    fwd.share(0)
    gg.own(0, 3)
    act(1)
    gg.oth(0, 1)
    act(2)
    gg.own(1, 4)
    fwd.share(1)
    gg.oth(1, 2)
    gg.own(0, 4)
    fwd.share(2)
    act(3)
    fwd.share(3)
    branch(1)
    gg.far(1, 3)
    gg.oth(0, 2)
    cot(0)
    branch(0)
    turn(0)
    out.hops(1, 4, 1)
    turn(1)
    gg.far(0, 3)
    gg.far(1, 4)
    cot(1)
    out.hops(0, 4, 1)
    gg.far(0, 4)
    out.hops(0, 4, 0)
    turn(2)
    out.hops(1, 4, 0)
    cot(2)
    turn(3)
    out.hops(1, 3, 1)
    cot(3)
    w_out.give(hid_t, cots)
    act_back(1)
    bwd.share(1)
    act_back(0)
    out.hops(1, 2, 1)
    bwd.share(0)
    act_back(2)
    out.hops(0, 3, 1)
    out.hops(1, 3, 0)
    out.hops(0, 3, 0)
    act_back(3)
    bwd.share(3)
    bwd.share(2)
    back_prod(1)
    out.hops(1, 1, 1)
    back_prod(0)
    out.hops(0, 2, 1)
    back.hops(1, 4, 0)
    out.hops(1, 2, 0)
    turn_back(1)
    back.hops(1, 4, 1)
    turn_back(0)
    back.hops(0, 4, 1)
    back.hops(0, 4, 0)
    turn_back(3)
    out.hops(0, 2, 0)
    out.cross(1)
    out.hops(0, 1, 1)
    turn_back(2)
    w_in.give(dpre_t, acts)
    back.hops(0, 3, 1)
    back.hops(1, 3, 1)
    back.hops(0, 3, 0)
    store_out_grad()
    back.hops(1, 3, 0)
    out.cross(0)
    back.hops(0, 2, 1)
    back.hops(1, 2, 1)
    out.hops(1, 1, 0)
    back.hops(0, 2, 0)
    back.hops(0, 1, 1)
    back.hops(1, 1, 1)
    back.hops(1, 2, 0)
    out.hops(0, 1, 0)
    out.rows(1)
    back.cross(0)
    back.hops(0, 1, 0)
    back.cross(1)
    back.hops(1, 1, 0)
    out.rows(0)
    back.rows(0)
    store_in_grad()
    back.rows(1)

    for copy in pending:
        copy.wait_send()
    for copy in (store_out, store_in, *out.keep.values(), *back.keep.values()):
        copy.wait()


def local(block_in, norm_gain, weight_in, weight_out, output_grad):
    hbm = pl.BlockSpec(memory_space=pl.ANY)
    rows, width = block_in.shape
    half = 2 * UNITS
    gain = norm_gain.reshape(1, width)

    def buf(*shape, dtype=BF16):
        return pltpu.VMEM(shape, dtype)

    quarter = BLOCK // NX
    inputs = dict(x=buf(rows, width), gain=buf(1, width, dtype=F32), g=buf(rows, width))
    scratch = dict(
        **inputs, wi=buf(NX, WIDE, UNITS), wo=buf(NX, UNITS, WIDE),
        msg=buf(NX, 2 * ROWS, WIDE), got=buf(NX, 2 * ROWS, WIDE),
        acts=buf(2, 32, CHUNK, SIDE), cots=buf(2, 32, CHUNK, SIDE),
        terms=buf(2, 4, NX, quarter, UNITS), terms_in=buf(2, 4, NX - 1, quarter, UNITS),
        slope=buf(4, quarter, UNITS, dtype=F32),
        hid=buf(4, NX, quarter, UNITS), dpre=buf(4, NX, quarter, UNITS),
        hid_t=buf(UNITS, 4 * BLOCK), dpre_t=buf(UNITS, 4 * BLOCK),
        prod=buf(2, 2, 2, 2 * NZ, UNIT, WIDE), prod_sib=buf(2, 2, 2 * NZ, UNIT, WIDE),
        ring_in=buf(2, 2, 2, 4, 2, UNIT, WIDE), ring_out=buf(2, 2, 2, 4, 2, UNIT, WIDE),
        y_out=buf(2, 2, UNIT, WIDE), y_in=buf(2, 2, UNIT, WIDE),
        rows_out=buf(2, NX, ROWS, WIDE, dtype=F32),
        gsum=buf(2, 2, UNITS, half, dtype=F32), gsend=buf(2, UNITS, half),
        gin_got=buf(2, UNITS, half), gres=buf(2, UNITS, half, dtype=F32),
        ssem=pltpu.SemaphoreType.DMA((SEMS,)), rsem=pltpu.SemaphoreType.DMA((SEMS,)),
        lsem=pltpu.SemaphoreType.DMA((13,)), ksem=pltpu.SemaphoreType.DMA((2, 2)),
    )
    summed, gin_t, gout = pl.pallas_call(
        kernel,
        name="block",
        out_shape=(
            jax.ShapeDtypeStruct((2, NX, rows, WIDE), F32),
            jax.ShapeDtypeStruct((UNITS, half), F32),
            jax.ShapeDtypeStruct((UNITS, half), F32),
        ),
        in_specs=[hbm] * 5,
        out_specs=(hbm,) * 3,
        scratch_shapes=list(scratch.values()),
        compiler_params=pltpu.CompilerParams(
            collective_id=0, has_side_effects=True, vmem_limit_bytes=VMEM_ASKED
        ),
    )(block_in, gain, weight_in, weight_out, output_grad)
    return pl.pallas_call(
        finish_kernel,
        name="finish",
        out_shape=(
            jax.ShapeDtypeStruct((rows, width), BF16),
            jax.ShapeDtypeStruct((rows, width), BF16),
            jax.ShapeDtypeStruct((half, UNITS), F32),
            jax.ShapeDtypeStruct((UNITS, half), F32),
        ),
        in_specs=[hbm] * 6,
        out_specs=(hbm,) * 4,
        scratch_shapes=[
            *inputs.values(), buf(2, NX, rows, WIDE, dtype=F32), buf(UNITS, half, dtype=F32),
            buf(half, UNITS, dtype=F32), buf(UNITS, half, dtype=F32), buf(rows, width),
            buf(rows, width), pltpu.SemaphoreType.DMA((6,)), pltpu.SemaphoreType.DMA((4,)),
        ],
        compiler_params=pltpu.CompilerParams(vmem_limit_bytes=VMEM_ASKED),
    )(block_in, gain, output_grad, summed, gin_t, gout)


def solution(mesh):
    in_specs = (P(("dp", "mp"), None), P(), P(None, "mp"), P("mp", None), P(("dp", "mp"), None))
    out_specs = (P(("dp", "mp"), None), P(("dp", "mp"), None), P("dp", "mp"), P("mp", "dp"))
    return jax.shard_map(local, mesh=mesh, in_specs=in_specs, out_specs=out_specs, check_vma=False)
```
